256 devices in a mesh: prow: 8 (over z), pcol: 32 (over x, y, core).
Axes of the slice: x: 4, y: 4, z: 8, core: 2. Of those that a mesh axis runs over, the one named last changes fastest.
Arguments:
- matrix: bfloat16 [6, 4096, 2, 16384], P(None, 'prow', None, 'pcol'), may hold values from -6 to 6
- diag_inverses: bfloat16 [512, 512], P('prow', 'pcol'), may hold values from -2 to 2, as said below
Outputs:
- updated: bfloat16 [6, 4096, 2, 16384], P(None, 'prow', None, 'pcol')
The draws below stay inside these ranges and needn't reach their ends.
Inputs may be any that keep to these rules, and one draw needn't show every extreme that they name: `diag_inverses`: strictly below the diagonal: the off-diagonal part of the inverse of a unit lower factor; on and above: the inverse of an upper factor, whose diagonal entries have magnitudes between 1 / sqrt(512) and 2 / sqrt(512).
All inputs are finite; a program needn't handle non-finite values.
Results may differ from the reference program's by a relative error of at most 0.0055.
Values may be sent and summed in bfloat16 or wider, within the bound.
A program may use at most 64 MiB of HBM per device.

```python
import jax
import jax.numpy as jnp
from jax import lax

NB = 512
ROWB_DEV = 6
COLB_DEV = 2
N_PROW = 8
N_PCOL = 32


def draw_diag_inverses(key, part):
    first, second, third = jax.random.split(jax.random.fold_in(key, 7), 3)
    offdiag = jnp.clip(jax.random.normal(first, (NB, NB), jnp.float32), -5.0, 5.0)
    magnitude = jax.random.uniform(second, (NB,), jnp.float32, 1.0, 2.0)
    signs = jnp.where(jax.random.uniform(third, (NB,), jnp.float32) < 0.5, -1.0, 1.0)
    row_index = jnp.arange(NB)[:, None]
    col_index = jnp.arange(NB)[None, :]
    scale_root = jnp.float32(NB) ** (-0.5)
    values = jnp.where(col_index < row_index, offdiag * scale_root, offdiag * scale_root * scale_root)
    diagonal = jnp.diag(signs * magnitude * scale_root)
    values = jnp.where(col_index == row_index, diagonal, values)
    return values.astype(jnp.bfloat16)


def level_of(rng, extent, shards, least, high):
    factor_of, own = 1.0, jax.random.fold_in(rng, 6)
    for position, shards_of in shards:
        steps = jnp.exp(jax.random.uniform(jax.random.fold_in(own, position), (shards_of,), jnp.float32, least / len(shards), high / len(shards)))
        factor_of = factor_of * jnp.repeat(steps, extent[position] // shards_of).reshape([-1 if axis == position else 1 for axis in range(len(extent))])
    return factor_of


def bell_draw(stream_key, extent, spread, bound, pieces=(), kind=jnp.bfloat16):
    values = jax.random.normal(stream_key, extent, jnp.float32) * spread
    if len(pieces) > 0:
        values = level_of(stream_key, extent, pieces, -0.22, 0.18) * values
    return jnp.clip(values, min=-bound, max=bound).astype(kind)


def setup_inputs(seed: int = 0) -> dict:
    streams_of = jax.random.split(jax.random.key(seed), 3)
    return {
        "matrix": bell_draw(streams_of[0], (ROWB_DEV, N_PROW * NB, COLB_DEV, N_PCOL * NB), 1.0, 6.0, ((1, 8), (3, 32))),
        "diag_inverses": draw_diag_inverses(jax.random.fold_in(streams_of[2], 71), 0),
    }


def reference(matrix, diag_inverses):
    width = diag_inverses.shape[0]
    total_rows = matrix.shape[0] * matrix.shape[1]
    total_cols = matrix.shape[2] * matrix.shape[3]
    full = matrix.reshape(total_rows, total_cols)
    row_index = jnp.arange(width, dtype=jnp.int32)[:, None]
    col_index = jnp.arange(width, dtype=jnp.int32)[None, :]
    zero_bf = jnp.zeros((width, width), diag_inverses.dtype)
    one_bf = jnp.ones((width, width), diag_inverses.dtype)
    lower_inv = jnp.where(col_index < row_index, diag_inverses, zero_bf)
    lower_inv = jnp.where(col_index == row_index, one_bf, lower_inv)
    upper_inv = jnp.where(col_index >= row_index, diag_inverses, zero_bf)
    l_panel = jnp.dot(full[width:, :width], upper_inv, preferred_element_type=jnp.float32).astype(matrix.dtype)
    u_panel = jnp.dot(lower_inv, full[:width, width:], preferred_element_type=jnp.float32).astype(matrix.dtype)
    blocks_below = (total_rows - width) // width
    lower_rows = full[width:, width:].reshape(blocks_below, width, total_cols - width)
    l_blocks = l_panel.reshape(blocks_below, width, width)

    def update_block(pair):
        rows_a, rows_l = pair
        product = jnp.dot(rows_l, u_panel, preferred_element_type=jnp.float32)
        return (rows_a.astype(jnp.float32) - product).astype(matrix.dtype)

    trailing = lax.map(update_block, (lower_rows, l_blocks)).reshape(total_rows - width, total_cols - width)
    head_rows = jnp.concatenate([full[:width, :width], u_panel], axis=1)
    tail_rows = jnp.concatenate([l_panel, trailing], axis=1)
    result = jnp.concatenate([head_rows, tail_rows], axis=0)
    return result.reshape(matrix.shape)
```

```python
import jax
import jax.numpy as jnp
from jax import lax
from jax.experimental import pallas as pl
from jax.experimental.pallas import tpu as pltpu
from jax.sharding import PartitionSpec as P

MESH = pl.DeviceIdType.MESH
BF16, F32 = jnp.bfloat16, jnp.float32
NB = 512
ROWS = 6 * NB
NZ = 8
STEPS = 16
LCH = ROWS // (4 * STEPS)
UCH = 64
BLK = 256


def parent(tree, node):
    bit = 1 << tree
    if not node & bit:
        return node | bit
    if node == bit:
        return 0
    for step in range(1, 4):
        other = 1 << ((tree + step) % 4)
        if node & other:
            return node ^ other


def depth(tree, node):
    return 0 if node == 0 else 1 + depth(tree, parent(tree, node))


def table(bits):
    return sum(1 << node for node in range(16) if bits(node))


CHILD = [[table(lambda v: v ^ (1 << j) and parent(i, v ^ (1 << j)) == v) for j in range(4)] for i in range(4)]
DEPTH = [[table(lambda v: (depth(i, v) >> b) & 1) for b in range(3)] for i in range(4)]


def gray_position(code):
    return code ^ (code >> 1)


def block_column(block):
    core, node = divmod(block, 16)
    return gray_position(node % 4) * 8 + gray_position(node // 4) * 2 + core


def kernel(a_hbm, d_ref, out_ref, av, sf, lraw, uraw, ub, uinv, linv, dz, dt, dtf,
           a_sem, l_send, l_recv, s_send, u_send, u_recv, z_send, z_recv, d_send, d_recv):
    z = lax.axis_index("prow")
    col = lax.axis_index("pcol")
    core = col % 2
    gx, gy = col // 8, (col // 2) % 4
    gx = gx ^ (gx >> 1)
    gy = gy ^ (gy >> 1)
    node = gx + 4 * gy
    sibling = col + 1 - 2 * core
    source = col == 0

    def near(dim):
        px, py = (gx ^ (1 << dim), gy) if dim < 2 else (gx, gy ^ (1 << (dim - 2)))
        return (px ^ (px >> 1)) * 8 + (py ^ (py >> 1)) * 2 + core

    nears = [near(dim) for dim in range(4)]

    def look(first, second):
        return (jnp.where(core == 0, first, second) >> node) & 1

    def load_a(piece):
        rows = pl.ds(pl.multiple_of(piece * (NB * 8), NB * 8), NB * 8)
        return pltpu.make_async_copy(a_hbm.at[rows], av.at[rows], a_sem.at[piece])

    for piece in range(6):
        load_a(piece).start()

    barrier = pltpu.get_barrier_semaphore()
    for step in range(1, NZ):
        pl.semaphore_signal(barrier, inc=1, device_id=((z + step) % NZ, col), device_id_type=MESH)
    for other in nears + [sibling]:
        pl.semaphore_signal(barrier, inc=1, device_id=(z, other), device_id_type=MESH)
    pl.semaphore_wait(barrier, NZ + 4)

    def z_copy(step):
        return pltpu.make_async_remote_copy(
            src_ref=d_ref, dst_ref=dz.at[z], send_sem=z_send.at[step - 1], recv_sem=z_recv.at[step - 1],
            device_id=((z + step) % NZ, col), device_id_type=MESH)

    for step in range(1, NZ):
        z_copy(step).start()
    dz[z] = d_ref[...]

    def d_copy(dim):
        if dim < 4:
            base = core * 16 + (node // (1 << dim)) * (1 << dim)
            blocks, target = pl.ds(base, 1 << dim), nears[dim]
        else:
            blocks, target = pl.ds(core * 16, 16), sibling
        return pltpu.make_async_remote_copy(
            src_ref=dt.at[blocks], dst_ref=dt.at[blocks], send_sem=d_send.at[dim], recv_sem=d_recv.at[dim],
            device_id=(z, target), device_id_type=MESH)

    def u_chunk(way, chunk):
        rows = pl.ds(pl.multiple_of((chunk % 8) * UCH, UCH), UCH)
        return uraw.at[2 * way + chunk // 8, rows]

    def u_copy(way, chunk):
        target = (z + 1) % NZ if way == 0 else (z + NZ - 1) % NZ
        part = u_chunk(way, chunk)
        return pltpu.make_async_remote_copy(
            src_ref=part, dst_ref=part, send_sem=u_send.at[way], recv_sem=u_recv.at[way, chunk],
            device_id=(target, col), device_id_type=MESH)

    def l_chunk(tree, chunk):
        return lraw.at[pl.ds(pl.multiple_of((chunk * 4 + tree) * LCH, LCH), LCH)]

    def l_copy(tree, chunk, target, sem):
        part = l_chunk(tree, chunk)
        return pltpu.make_async_remote_copy(
            src_ref=part, dst_ref=part, send_sem=sem, recv_sem=l_recv.at[tree, chunk],
            device_id=(z, target), device_id_type=MESH)

    def spread(first, rows):
        first = pl.multiple_of(first * 8, 16)
        sf[pl.ds(0, rows * 8), :] = av[pl.ds(first, rows * 8), :].astype(F32)

    hop_plus, hop_minus = z, (NZ - z) % NZ
    own, sends, hops = [], [], []
    for k in range(2):
        own.append(2 * core + k)
        sends.append([look(CHILD[k][dim], CHILD[2 + k][dim]) == 1 for dim in range(4)])
        hops.append(sum(look(DEPTH[k][b], DEPTH[2 + k][b]) << b for b in range(3)) + core)
    others, other_hops = [], []
    for k in range(2):
        tree = 2 * (1 - core) + k
        hop = sum(((jnp.where(core == 0, DEPTH[2 + k][b], DEPTH[k][b]) >> node) & 1) << b for b in range(3))
        others.append(tree)
        other_hops.append(jnp.where(source, 0, hop + (1 - core) + 1))
    root_second = (node == 0) & (core == 1)

    for piece in range(1):
        load_a(piece).wait()

    def step_body(g, carry):
        @pl.when((z == 0) & (g < 8))
        def _():
            spread(g * UCH, UCH)
            for t in range(4):
                for j in range(2):
                    x = sf[pl.ds(2 * t + j, UCH, stride=8), :].astype(BF16)
                    uraw[t, pl.ds(pl.multiple_of(g * UCH, UCH), UCH), j * 128:(j + 1) * 128] = x

        for way, hop in ((0, hop_plus), (1, hop_minus)):
            chunk = g - hop
            live = (chunk >= 0) & (chunk < STEPS)

            @pl.when(live & (z != 0))
            def _():
                u_copy(way, chunk).wait_recv()

            @pl.when(live & (hop != NZ - 1))
            def _():
                u_copy(way, chunk).start()

        @pl.when(source & (g < STEPS))
        def _():
            spread(g * 4 * LCH, 4 * LCH)
            for t in range(4):
                x = sf[pl.ds(2 * t, 4 * LCH, stride=8), :].astype(BF16)
                lraw[pl.ds(pl.multiple_of(g * 4 * LCH, 4 * LCH), 4 * LCH), t * 128:(t + 1) * 128] = x

        for k in range(2):
            chunk = g - hops[k]
            live = (chunk >= 0) & (chunk < STEPS)

            @pl.when(live & jnp.logical_not(source))
            def _():
                l_copy(own[k], chunk, sibling, s_send.at[k]).wait_recv()

            for dim in range(4):
                @pl.when(live & sends[k][dim])
                def _():
                    l_copy(own[k], chunk, nears[dim], l_send.at[k, dim]).start()

            @pl.when(live & jnp.logical_not(root_second))
            def _():
                l_copy(own[k], chunk, sibling, s_send.at[k]).start()

        for k in range(2):
            chunk = g - other_hops[k]
            live = (chunk >= 0) & (chunk < STEPS)

            @pl.when(live & jnp.logical_not(source))
            def _():
                l_copy(others[k], chunk, sibling, s_send.at[2 + k]).wait_recv()

            @pl.when(live & source)
            def _():
                l_copy(others[k], chunk, sibling, s_send.at[2 + k]).start()

        @pl.when(g == 1)
        def _():
            for step in range(1, NZ):
                z_copy(step).wait()
            dt[core * 16 + node] = jnp.concatenate([dz[i] for i in range(NZ)], axis=1)
            d_copy(0).start()

        for dim in range(1, 5):
            @pl.when(g == 1 + dim)
            def _():
                d_copy(dim - 1).wait()
                d_copy(dim).start()

        @pl.when((g >= 1) & (g < 6) & source)
        def _():
            load_a(g).wait()

        return carry

    lax.fori_loop(0, STEPS + NZ - 1, step_body, 0)

    d_copy(4).wait()

    @pl.when(jnp.logical_not(source))
    def _():
        for piece in range(1, 6):
            load_a(piece).wait()

    for way, hop in ((0, hop_plus), (1, hop_minus)):
        @pl.when(hop != NZ - 1)
        def _():
            part = uraw.at[pl.ds(2 * way, 2)]
            pltpu.make_async_copy(part, part, u_send.at[way]).wait()

    for k in range(2):
        part = lraw.at[pl.ds(0, STEPS * LCH)]
        for dim in range(4):
            @pl.when(sends[k][dim])
            def _():
                pltpu.make_async_copy(part, part, l_send.at[k, dim]).wait()

        @pl.when(jnp.logical_not(root_second))
        def _():
            pltpu.make_async_copy(part, part, s_send.at[k]).wait()

        @pl.when(source)
        def _():
            pltpu.make_async_copy(part, part, s_send.at[2 + k]).wait()

    for block in range(32):
        dtf[pl.ds(block_column(block) * 16, 16), :] = dt[block].astype(F32)
    packed = dtf[...].T
    row = lax.broadcasted_iota(jnp.int32, (NB, NB), 0)
    column = lax.broadcasted_iota(jnp.int32, (NB, NB), 1)
    uinv[...] = jnp.where(column >= row, packed, 0.0).astype(BF16)
    linv[...] = jnp.where(column < row, packed, jnp.where(column == row, 1.0, 0.0)).astype(BF16)

    for t in range(4):
        ub[t] = jnp.dot(linv[...], uraw[t], preferred_element_type=F32).astype(BF16)

    def update(b, carry):
        first = pl.multiple_of(b * BLK, BLK)
        head = (z == 0) & (b < NB // BLK)

        @pl.when(jnp.logical_not(head))
        def _():
            l = jnp.dot(lraw[pl.ds(first, BLK), :], uinv[...], preferred_element_type=F32).astype(BF16)
            for t in range(4):
                p = jnp.dot(l, ub[t], preferred_element_type=F32)
                for j in range(2):
                    sf[pl.ds(2 * t + j, BLK, stride=8), :] = p[:, j * 128:(j + 1) * 128]

            @pl.when(source)
            def _():
                for t in range(4):
                    sf[pl.ds(2 * t, BLK, stride=8), :] = -l[:, t * 128:(t + 1) * 128].astype(F32)

        @pl.when(head)
        def _():
            for t in range(4):
                for j in range(2):
                    u = ub[t, pl.ds(first, BLK), j * 128:(j + 1) * 128].astype(F32)
                    sf[pl.ds(2 * t + j, BLK, stride=8), :] = -u

            @pl.when(source)
            def _():
                for t in range(4):
                    sf[pl.ds(2 * t, BLK, stride=8), :] = jnp.zeros((BLK, 128), F32)

        keep_even = jnp.where(head == source, 1.0, 0.0)
        keep_odd = jnp.where(head, 0.0, 1.0)
        even = lax.broadcasted_iota(jnp.int32, (8, 128), 0) % 2 == 0
        keep = jnp.where(even, keep_even, keep_odd)
        rows = pl.ds(pl.multiple_of(first * 8, BLK * 8), BLK * 8)
        a = av[rows, :].astype(F32).reshape(BLK, 8, 128) * keep[None]
        out_ref[rows, :] = (a.reshape(BLK * 8, 128) - sf[...]).astype(BF16)
        return carry

    lax.fori_loop(0, ROWS // BLK, update, 0)


def settle(x_ref, out_ref, sem):
    parts = [pl.ds(piece * NB * 8, NB * 8) for piece in range(6)]
    copies = [pltpu.make_async_copy(x_ref.at[part], out_ref.at[part], sem.at[i]) for i, part in enumerate(parts)]
    for copy in copies:
        copy.start()
    for copy in copies:
        copy.wait()


def shards(matrix, diag_inverses):
    flat = matrix.reshape(ROWS, 2, 4, 128).transpose(0, 2, 1, 3).reshape(ROWS * 8, 128)
    dma = pltpu.SemaphoreType.DMA
    out = pl.pallas_call(
        kernel,
        out_shape=jax.ShapeDtypeStruct((ROWS * 8, 128), BF16),
        in_specs=[pl.BlockSpec(memory_space=pltpu.HBM), pl.BlockSpec(memory_space=pltpu.VMEM)],
        out_specs=pl.BlockSpec(memory_space=pltpu.VMEM),
        scratch_shapes=[
            pltpu.VMEM((ROWS * 8, 128), BF16),
            pltpu.VMEM((BLK * 8, 128), F32),
            pltpu.VMEM((ROWS, NB), BF16),
            pltpu.VMEM((4, NB, 256), BF16),
            pltpu.VMEM((4, NB, 256), BF16),
            pltpu.VMEM((NB, NB), BF16),
            pltpu.VMEM((NB, NB), BF16),
            pltpu.VMEM((NZ, 16, 64), BF16),
            pltpu.VMEM((32, 16, NB), BF16),
            pltpu.VMEM((NB, NB), F32),
            dma((6,)),
            dma((2, 4)),
            dma((4, STEPS)),
            dma((4,)),
            dma((2,)),
            dma((2, STEPS)),
            dma((NZ - 1,)),
            dma((NZ - 1,)),
            dma((5,)),
            dma((5,)),
        ],
        compiler_params=pltpu.CompilerParams(
            collective_id=0, has_side_effects=True, vmem_limit_bytes=32 * 2**20),
    )(flat, diag_inverses.T)
    out = pl.pallas_call(
        settle,
        out_shape=jax.ShapeDtypeStruct((ROWS * 8, 128), BF16),
        in_specs=[pl.BlockSpec(memory_space=pl.ANY)],
        out_specs=pl.BlockSpec(memory_space=pl.ANY),
        scratch_shapes=[dma((6,))],
        compiler_params=pltpu.CompilerParams(vmem_limit_bytes=2**20),
    )(out)
    return out.reshape(ROWS, 4, 2, 128).transpose(0, 2, 1, 3).reshape(matrix.shape)


def solution(mesh):
    in_specs = (P(None, "prow", None, "pcol"), P("prow", "pcol"))
    out_specs = P(None, "prow", None, "pcol")
    return jax.shard_map(shards, mesh=mesh, in_specs=in_specs, out_specs=out_specs, check_vma=False)
```

```python
import jax
import jax.numpy as jnp
from jax import lax
from jax.experimental import pallas as pl
from jax.experimental.pallas import tpu as pltpu
from jax.sharding import PartitionSpec as P

MESH = pl.DeviceIdType.MESH
BF16, F32 = jnp.bfloat16, jnp.float32
NB = 512
ROWS = 6 * NB
NZ = 8
STEPS = 16
LCH = ROWS // (4 * STEPS)
UCH = 64
UPER = NB // UCH
BLK = 256
UHOP, LHOP, CHOP = 6, 6, 3
SLOTS = 4
TOTAL = STEPS + (NZ - 1) * UHOP
DSTEP = 6
INVERT = DSTEP + 4 * LHOP + CHOP
EARLY = max(INVERT, STEPS + NZ // 2 * UHOP)
SOLVE = max(EARLY, 5 * LHOP + 2 * CHOP)
LATE = max(SOLVE + STEPS, UPER + (NZ - 1) * UHOP)
PER = -(-(ROWS // BLK) // (TOTAL - LATE))


def parent(tree, node):
    bit = 1 << tree
    if not node & bit:
        return node | bit
    if node == bit:
        return 0
    for step in range(1, 4):
        other = 1 << ((tree + step) % 4)
        if node & other:
            return node ^ other


def depth(tree, node):
    return 0 if node == 0 else 1 + depth(tree, parent(tree, node))


def table(bits):
    return sum(1 << node for node in range(16) if bits(node))


CHILD = [[table(lambda v: v ^ (1 << j) and parent(i, v ^ (1 << j)) == v) for j in range(4)] for i in range(4)]
DEPTH = [[table(lambda v: (depth(i, v) >> b) & 1) for b in range(3)] for i in range(4)]


def gray_position(code):
    return code ^ (code >> 1)


def block_column(block):
    core, node = divmod(block, 16)
    return gray_position(node % 4) * 8 + gray_position(node // 4) * 2 + core


def kernel(av, d_ref, s_ref, sf, lraw, lsol, uraw, ub, uinv, linv, dz, dt, dtf,
           l_send, l_recv, s_send, u_send, u_recv, z_send, z_recv, d_send, d_recv):
    z = lax.axis_index("prow")
    col = lax.axis_index("pcol")
    core = col % 2
    gx, gy = col // 8, (col // 2) % 4
    gx = gx ^ (gx >> 1)
    gy = gy ^ (gy >> 1)
    node = gx + 4 * gy
    sibling = col + 1 - 2 * core
    source = col == 0
    plain = col != 0

    def near(dim):
        px, py = (gx ^ (1 << dim), gy) if dim < 2 else (gx, gy ^ (1 << (dim - 2)))
        return (px ^ (px >> 1)) * 8 + (py ^ (py >> 1)) * 2 + core

    nears = [near(dim) for dim in range(4)]

    def look(first, second):
        return (jnp.where(core == 0, first, second) >> node) & 1

    barrier = pltpu.get_barrier_semaphore()
    for step in range(1, NZ):
        pl.semaphore_signal(barrier, inc=1, device_id=((z + step) % NZ, col), device_id_type=MESH)
    for other in nears + [sibling]:
        pl.semaphore_signal(barrier, inc=1, device_id=(z, other), device_id_type=MESH)
    pl.semaphore_wait(barrier, NZ + 4)

    def z_copy(step):
        return pltpu.make_async_remote_copy(
            src_ref=d_ref, dst_ref=dz.at[z], send_sem=z_send.at[step - 1], recv_sem=z_recv.at[step - 1],
            device_id=((z + step) % NZ, col), device_id_type=MESH)

    def d_copy(dim):
        if dim < 4:
            base = core * 16 + (node // (1 << dim)) * (1 << dim)
            blocks, target = pl.ds(base, 1 << dim), nears[dim]
        else:
            blocks, target = pl.ds(core * 16, 16), sibling
        return pltpu.make_async_remote_copy(
            src_ref=dt.at[blocks], dst_ref=dt.at[blocks], send_sem=d_send.at[dim], recv_sem=d_recv.at[dim],
            device_id=(z, target), device_id_type=MESH)

    def u_copy(way, chunk):
        target = (z + 1) % NZ if way == 0 else (z + NZ - 1) % NZ
        rows = pl.ds(pl.multiple_of(lax.rem(chunk, UPER) * UCH, UCH), UCH)
        part = uraw.at[2 * way + lax.div(chunk, UPER), rows]
        return pltpu.make_async_remote_copy(
            src_ref=part, dst_ref=part, send_sem=u_send.at[way, lax.rem(chunk, SLOTS)], recv_sem=u_recv.at[way, chunk],
            device_id=(target, col), device_id_type=MESH)

    def l_copy(tree, chunk, target, sem):
        part = lraw.at[pl.ds(pl.multiple_of((chunk * 4 + tree) * LCH, LCH), LCH)]
        return pltpu.make_async_remote_copy(
            src_ref=part, dst_ref=part, send_sem=sem.at[lax.rem(chunk, SLOTS)], recv_sem=l_recv.at[tree, chunk],
            device_id=(z, target), device_id_type=MESH)

    def push(tree, chunk, target, sem):
        @pl.when(chunk >= SLOTS)
        def _():
            l_copy(tree, chunk - SLOTS, target, sem).wait_send()

        l_copy(tree, chunk, target, sem).start()

    def spread(first, rows):
        first = pl.multiple_of(first * 8, 16)
        sf[pl.ds(0, rows * 8), :] = av[pl.ds(first, rows * 8), :].astype(F32)

    hop_plus, hop_minus = z, (NZ - z) % NZ
    own, sends, hops = [], [], []
    others, other_hops = [], []
    for k in range(2):
        own.append(2 * core + k)
        sends.append([look(CHILD[k][dim], CHILD[2 + k][dim]) == 1 for dim in range(4)])
        hops.append(sum(look(DEPTH[k][b], DEPTH[2 + k][b]) << b for b in range(3)) * LHOP + core * CHOP)
        others.append(2 * (1 - core) + k)
        hop = sum(look(DEPTH[2 + k][b], DEPTH[k][b]) << b for b in range(3))
        other_hops.append(jnp.where(source, 0, hop * LHOP + (2 - core) * CHOP))
    to_sibling = jnp.logical_not((node == 0) & (core == 1))
    near_t = jnp.where(z <= NZ // 2, 0, 2)
    far_t = 2 - near_t

    def solve_u(t):
        ub[t] = jnp.dot(linv[...], uraw[t], preferred_element_type=F32).astype(BF16)

    def update(t, first, rows, l):
        p = jnp.dot(l, ub[t], preferred_element_type=F32)
        base = first * 8 + 2 * t

        @pl.when(plain)
        def _():
            s_ref[pl.ds(base, rows, stride=8), :] = p[:, 0:128]

        s_ref[pl.ds(base + 1, rows, stride=8), :] = p[:, 128:256]

    def update_block(t, b):
        first = pl.multiple_of(b * BLK, BLK)
        update(t, first, BLK, lsol[pl.ds(first, BLK), :])

    def step_body(g, carry):
        @pl.when((z == 0) & (g < UPER))
        def _():
            spread(g * UCH, UCH)
            for t in range(4):
                for j in range(2):
                    x = sf[pl.ds(2 * t + j, UCH, stride=8), :].astype(BF16)
                    uraw[t, pl.ds(pl.multiple_of(g * UCH, UCH), UCH), j * 128:(j + 1) * 128] = x

        for way, hop in ((0, hop_plus), (1, hop_minus)):
            chunk = g - hop * UHOP

            @pl.when((chunk >= 0) & (chunk < STEPS))
            def _():
                @pl.when(z != 0)
                def _():
                    u_copy(way, chunk).wait_recv()

                @pl.when(hop != NZ - 1)
                def _():
                    @pl.when(chunk >= SLOTS)
                    def _():
                        u_copy(way, chunk - SLOTS).wait_send()

                    u_copy(way, chunk).start()

        @pl.when(source & (g < STEPS))
        def _():
            spread(g * 4 * LCH, 4 * LCH)
            for t in range(4):
                x = sf[pl.ds(2 * t, 4 * LCH, stride=8), :].astype(BF16)
                lraw[pl.ds(pl.multiple_of(g * 4 * LCH, 4 * LCH), 4 * LCH), t * 128:(t + 1) * 128] = x

        for k in range(2):
            chunk = g - hops[k]

            @pl.when((chunk >= 0) & (chunk < STEPS))
            def _():
                @pl.when(plain)
                def _():
                    l_copy(own[k], chunk, sibling, s_send.at[k]).wait_recv()

                for dim in range(4):
                    @pl.when(sends[k][dim])
                    def _():
                        push(own[k], chunk, nears[dim], l_send.at[k, dim])

                @pl.when(to_sibling)
                def _():
                    push(own[k], chunk, sibling, s_send.at[k])

        for k in range(2):
            chunk = g - other_hops[k]

            @pl.when((chunk >= 0) & (chunk < STEPS))
            def _():
                @pl.when(plain)
                def _():
                    l_copy(others[k], chunk, sibling, s_send.at[2 + k]).wait_recv()

                @pl.when(source)
                def _():
                    push(others[k], chunk, sibling, s_send.at[2 + k])

        @pl.when(g <= INVERT)
        def _():
            @pl.when(g == 0)
            def _():
                for step in range(1, NZ):
                    z_copy(step).start()
                dz[z] = d_ref[...]

            @pl.when(g == DSTEP)
            def _():
                for step in range(1, NZ):
                    z_copy(step).wait()
                dt[core * 16 + node] = jnp.concatenate([dz[i] for i in range(NZ)], axis=1)
                d_copy(0).start()

            for dim in range(1, 5):
                @pl.when(g == DSTEP + LHOP * dim)
                def _():
                    d_copy(dim - 1).wait()
                    d_copy(dim).start()

            @pl.when(g == INVERT)
            def _():
                d_copy(4).wait()
                for block in range(32):
                    dtf[pl.ds(block_column(block) * 16, 16), :] = dt[block].astype(F32)
                packed = dtf[...].T
                row = lax.broadcasted_iota(jnp.int32, (NB, NB), 0)
                column = lax.broadcasted_iota(jnp.int32, (NB, NB), 1)
                uinv[...] = jnp.where(column >= row, packed, 0.0).astype(BF16)
                linv[...] = jnp.where(column < row, packed, jnp.where(column == row, 1.0, 0.0)).astype(BF16)

        @pl.when(g == EARLY)
        def _():
            solve_u(near_t)
            solve_u(near_t + 1)

        @pl.when((g >= SOLVE) & (g < SOLVE + STEPS))
        def _():
            first = pl.multiple_of((g - SOLVE) * 4 * LCH, 4 * LCH)
            rows = pl.ds(first, 4 * LCH)
            l = jnp.dot(lraw[rows, :], uinv[...], preferred_element_type=F32).astype(BF16)
            lsol[rows, :] = l
            update(near_t, first, 4 * LCH, l)
            update(near_t + 1, first, 4 * LCH, l)

            @pl.when(source)
            def _():
                for t in range(4):
                    s_ref[pl.ds(first * 8 + 2 * t, 4 * LCH, stride=8), :] = -l[:, t * 128:(t + 1) * 128].astype(F32)

        @pl.when(g >= LATE)
        def _():
            @pl.when(g == LATE)
            def _():
                solve_u(far_t)

            for i in range(PER):
                b = (g - LATE) * PER + i

                @pl.when(b < ROWS // BLK)
                def _():
                    update_block(far_t, b)

        return carry

    lax.fori_loop(0, TOTAL, step_body, 0)

    solve_u(far_t + 1)

    def last_body(b, carry):
        update_block(far_t + 1, b)
        return carry

    lax.fori_loop(0, ROWS // BLK, last_body, 0)

    @pl.when(z == 0)
    def _():
        for t in range(4):
            s_ref[pl.ds(2 * t, NB, stride=8), :] = jnp.where(source, 0.0, -ub[t, :, 0:128].astype(F32))
            s_ref[pl.ds(2 * t + 1, NB, stride=8), :] = -ub[t, :, 128:256].astype(F32)

    def drain(last, carry):
        for way, hop in ((0, hop_plus), (1, hop_minus)):
            @pl.when(hop != NZ - 1)
            def _():
                u_copy(way, last).wait_send()

        for k in range(2):
            for dim in range(4):
                @pl.when(sends[k][dim])
                def _():
                    l_copy(own[k], last, nears[dim], l_send.at[k, dim]).wait_send()

            @pl.when(to_sibling)
            def _():
                l_copy(own[k], last, sibling, s_send.at[k]).wait_send()

            @pl.when(source)
            def _():
                l_copy(others[k], last, sibling, s_send.at[2 + k]).wait_send()

        return carry

    lax.fori_loop(STEPS - SLOTS, STEPS, drain, 0)


def settle(s_ref, a_ref, out_ref, buf, sem):
    z = lax.axis_index("prow")
    source = lax.axis_index("pcol") == 0
    even = lax.broadcasted_iota(jnp.int32, (8, 128), 0) % 2 == 0
    size = BLK * 8

    def copy(b):
        rows = pl.ds(pl.multiple_of(b * size, size), size)
        return pltpu.make_async_copy(buf.at[rows], out_ref.at[rows], sem.at[b])

    def body(b, carry):
        head = (z == 0) & (b < NB // BLK)
        keep_even = jnp.where(head == source, 1.0, 0.0)
        keep_odd = jnp.where(head, 0.0, 1.0)
        keep = jnp.where(even, keep_even, keep_odd)
        rows = pl.ds(pl.multiple_of(b * size, size), size)
        a = a_ref[rows, :].astype(F32).reshape(BLK, 8, 128) * keep[None]
        buf[rows, :] = (a.reshape(size, 128) - s_ref[rows, :]).astype(BF16)
        copy(b).start()
        return carry

    def finish(b, carry):
        copy(b).wait()
        return carry

    lax.fori_loop(0, ROWS // BLK, body, 0)
    lax.fori_loop(0, ROWS // BLK, finish, 0)


def shards(matrix, diag_inverses):
    flat = matrix.reshape(ROWS, 2, 4, 128).transpose(0, 2, 1, 3).reshape(ROWS * 8, 128)
    dma = pltpu.SemaphoreType.DMA
    vmem = pl.BlockSpec(memory_space=pltpu.VMEM)
    product = pl.pallas_call(
        kernel,
        out_shape=jax.ShapeDtypeStruct((ROWS * 8, 128), F32),
        in_specs=[vmem, vmem],
        out_specs=vmem,
        scratch_shapes=[
            pltpu.VMEM((4 * LCH * 8, 128), F32),
            pltpu.VMEM((ROWS, NB), BF16),
            pltpu.VMEM((ROWS, NB), BF16),
            pltpu.VMEM((4, NB, 256), BF16),
            pltpu.VMEM((4, NB, 256), BF16),
            pltpu.VMEM((NB, NB), BF16),
            pltpu.VMEM((NB, NB), BF16),
            pltpu.VMEM((NZ, 16, 64), BF16),
            pltpu.VMEM((32, 16, NB), BF16),
            pltpu.VMEM((NB, NB), F32),
            dma((2, 4, SLOTS)),
            dma((4, STEPS)),
            dma((4, SLOTS)),
            dma((2, SLOTS)),
            dma((2, STEPS)),
            dma((NZ - 1,)),
            dma((NZ - 1,)),
            dma((5,)),
            dma((5,)),
        ],
        compiler_params=pltpu.CompilerParams(
            collective_id=0, has_side_effects=True, vmem_limit_bytes=20 * 2**20),
    )(flat, diag_inverses.T)
    out = pl.pallas_call(
        settle,
        out_shape=jax.ShapeDtypeStruct((ROWS * 8, 128), BF16),
        in_specs=[vmem, vmem],
        out_specs=pl.BlockSpec(memory_space=pl.ANY),
        scratch_shapes=[pltpu.VMEM((ROWS * 8, 128), BF16), dma((ROWS // BLK,))],
        compiler_params=pltpu.CompilerParams(vmem_limit_bytes=12 * 2**20),
    )(product, flat)
    return out.reshape(ROWS, 4, 2, 128).transpose(0, 2, 1, 3).reshape(matrix.shape)


def solution(mesh):
    in_specs = (P(None, "prow", None, "pcol"), P("prow", "pcol"))
    out_specs = P(None, "prow", None, "pcol")
    return jax.shard_map(shards, mesh=mesh, in_specs=in_specs, out_specs=out_specs, check_vma=False)
```

```python
import functools

import jax
import jax.numpy as jnp
from jax import lax
from jax.experimental import pallas as pl
from jax.experimental.pallas import tpu as pltpu
from jax.sharding import PartitionSpec as P

MESH = pl.DeviceIdType.MESH
BF16, F32 = jnp.bfloat16, jnp.float32
NB = 512
ROWS = 6 * NB
NZ = 8
STEPS = 16
LSTEPS = 12
LCH = ROWS // (4 * LSTEPS)
UCH = 2 * NB // STEPS
UPER = NB // UCH
BLK = 512
UHOP, LHOP, CHOP = 6, 6, 3
JUMP = 7
SLOTS = 4
TOTAL = max(UPER + (NZ - 1) * UHOP, STEPS + 3 * JUMP + UHOP)
DSTEP, DHOP = 4, 4
INVERT = DSTEP + 4 * DHOP + 2
PAIR = 8 * LCH
OUT = 256
PER = 3


def parent(tree, node):
    bit = 1 << tree
    if not node & bit:
        return node | bit
    if node == bit:
        return 0
    for step in range(1, 4):
        other = 1 << ((tree + step) % 4)
        if node & other:
            return node ^ other


def depth(tree, node):
    return 0 if node == 0 else 1 + depth(tree, parent(tree, node))


def table(bits):
    return sum(1 << node for node in range(16) if bits(node))


CHILD = [[table(lambda v: v ^ (1 << j) and parent(i, v ^ (1 << j)) == v) for j in range(4)] for i in range(4)]
DEPTH = [[table(lambda v: (depth(i, v) >> b) & 1) for b in range(3)] for i in range(4)]


def gray_position(code):
    return code ^ (code >> 1)


def block_column(block):
    core, node = divmod(block, 16)
    return gray_position(node % 4) * 8 + gray_position(node // 4) * 2 + core


def kernel(av, d_ref, s_ref, sf, lraw, lsol, uraw, ub, uinv, linv, dz, dt, dtf,
           l_send, l_recv, s_send, u_send, u_recv, z_send, z_recv, d_send, d_recv):
    z = lax.axis_index("prow")
    col = lax.axis_index("pcol")
    core = col % 2
    gx, gy = col // 8, (col // 2) % 4
    gx = gx ^ (gx >> 1)
    gy = gy ^ (gy >> 1)
    node = gx + 4 * gy
    sibling = col + 1 - 2 * core
    source = col == 0
    plain = col != 0

    def near(dim):
        px, py = (gx ^ (1 << dim), gy) if dim < 2 else (gx, gy ^ (1 << (dim - 2)))
        return (px ^ (px >> 1)) * 8 + (py ^ (py >> 1)) * 2 + core

    nears = [near(dim) for dim in range(4)]

    def look(first, second):
        return (jnp.where(core == 0, first, second) >> node) & 1

    barrier = pltpu.get_barrier_semaphore()
    for step in range(1, NZ):
        pl.semaphore_signal(barrier, inc=1, device_id=((z + step) % NZ, col), device_id_type=MESH)
    for other in nears + [sibling]:
        pl.semaphore_signal(barrier, inc=1, device_id=(z, other), device_id_type=MESH)
    pl.semaphore_wait(barrier, NZ + 4)

    def z_copy(step):
        return pltpu.make_async_remote_copy(
            src_ref=d_ref, dst_ref=dz.at[z], send_sem=z_send.at[step - 1], recv_sem=z_recv.at[step - 1],
            device_id=((z + step) % NZ, col), device_id_type=MESH)

    def d_copy(dim):
        if dim < 4:
            base = core * 16 + (node // (1 << dim)) * (1 << dim)
            blocks, target = pl.ds(base, 1 << dim), nears[dim]
        else:
            blocks, target = pl.ds(core * 16, 16), sibling
        return pltpu.make_async_remote_copy(
            src_ref=dt.at[blocks], dst_ref=dt.at[blocks], send_sem=d_send.at[dim], recv_sem=d_recv.at[dim],
            device_id=(z, target), device_id_type=MESH)

    def u_copy(way, chunk, ahead=1, kind=0):
        target = (z + ahead) % NZ if way == 0 else (z + NZ - ahead) % NZ
        rows = pl.ds(pl.multiple_of(lax.rem(chunk, UPER) * UCH, UCH), UCH)
        part = uraw.at[2 * way + lax.div(chunk, UPER), rows]
        return pltpu.make_async_remote_copy(
            src_ref=part, dst_ref=part, send_sem=u_send.at[kind, way, lax.rem(chunk, SLOTS)], recv_sem=u_recv.at[way, chunk],
            device_id=(target, col), device_id_type=MESH)

    def l_copy(tree, chunk, target, sem):
        part = lraw.at[pl.ds(pl.multiple_of((chunk * 4 + tree) * LCH, LCH), LCH)]
        return pltpu.make_async_remote_copy(
            src_ref=part, dst_ref=part, send_sem=sem.at[lax.rem(chunk, SLOTS)], recv_sem=l_recv.at[tree, chunk],
            device_id=(z, target), device_id_type=MESH)

    def push(tree, chunk, target, sem):
        @pl.when(chunk >= SLOTS)
        def _():
            l_copy(tree, chunk - SLOTS, target, sem).wait_send()

        l_copy(tree, chunk, target, sem).start()

    def spread(first, rows):
        first = pl.multiple_of(first * 8, 16)
        sf[pl.ds(0, rows * 8), :] = av[pl.ds(first, rows * 8), :].astype(F32)

    hop_plus, hop_minus = z, (NZ - z) % NZ
    ways = ((0, hop_plus), (1, hop_minus))

    def skip_delay(hop):
        jumps = jnp.where(hop == NZ - 1, 3, lax.div(hop + 1, 2))
        return jumps * JUMP + lax.rem(hop, 2) * UHOP

    own, sends, hops = [], [], []
    others, other_hops = [], []
    for k in range(2):
        own.append(2 * core + k)
        sends.append([look(CHILD[k][dim], CHILD[2 + k][dim]) == 1 for dim in range(4)])
        hops.append(sum(look(DEPTH[k][b], DEPTH[2 + k][b]) << b for b in range(3)) * LHOP + core * CHOP)
        others.append(2 * (1 - core) + k)
        hop = sum(look(DEPTH[2 + k][b], DEPTH[k][b]) << b for b in range(3))
        other_hops.append(jnp.where(source, 0, hop * LHOP + (2 - core) * CHOP))
    to_sibling = jnp.logical_not((node == 0) & (core == 1))
    near_hop = jnp.minimum(hop_plus, hop_minus)
    early = jnp.maximum(INVERT, jnp.maximum(UPER + near_hop * UHOP, STEPS + skip_delay(near_hop)))
    solve = jnp.maximum(early, functools.reduce(jnp.maximum, hops + other_hops))
    late = jnp.maximum(solve + LSTEPS, STEPS + skip_delay(jnp.maximum(hop_plus, hop_minus)))
    near_t = jnp.where(z <= NZ // 2, 0, 2)
    far_t = 2 - near_t

    def solve_u(t):
        ub[t] = jnp.dot(linv[...], uraw[t], preferred_element_type=F32).astype(BF16)

    def update(t, first, rows, l):
        p = jnp.dot(l, ub[t], preferred_element_type=F32)
        base = first * 8 + 2 * t

        @pl.when(plain)
        def _():
            s_ref[pl.ds(base, rows, stride=8), :] = p[:, 0:128]

        s_ref[pl.ds(base + 1, rows, stride=8), :] = p[:, 128:256]

    def update_block(t, b):
        first = pl.multiple_of(b * BLK, BLK)
        update(t, first, BLK, lsol[pl.ds(first, BLK), :])

    def step_body(g, carry):
        @pl.when((z == 0) & (g < UPER))
        def _():
            spread(g * UCH, UCH)
            for t in range(4):
                for j in range(2):
                    x = sf[pl.ds(2 * t + j, UCH, stride=8), :].astype(BF16)
                    uraw[t, pl.ds(pl.multiple_of(g * UCH, UCH), UCH), j * 128:(j + 1) * 128] = x

        for way, hop in ways:
            chunk = g - hop * UHOP

            @pl.when((chunk >= 0) & (chunk < UPER))
            def _():
                @pl.when(z != 0)
                def _():
                    u_copy(way, chunk).wait_recv()

                @pl.when(hop != NZ - 1)
                def _():
                    @pl.when(chunk >= SLOTS)
                    def _():
                        u_copy(way, chunk - SLOTS).wait_send()

                    u_copy(way, chunk).start()

            skip = g - skip_delay(hop)

            @pl.when((skip >= UPER) & (skip < STEPS))
            def _():
                @pl.when(z != 0)
                def _():
                    u_copy(way, skip).wait_recv()

                @pl.when(lax.rem(hop, 2) == 0)
                def _():
                    ahead = jnp.where(hop == NZ - 2, 1, 2)

                    @pl.when(skip >= UPER + SLOTS)
                    def _():
                        u_copy(way, skip - SLOTS, ahead, 1).wait_send()

                    u_copy(way, skip, ahead, 1).start()

                    @pl.when(hop != 0)
                    def _():
                        @pl.when(skip >= UPER + SLOTS)
                        def _():
                            u_copy(way, skip - SLOTS, NZ - 1, 2).wait_send()

                        u_copy(way, skip, NZ - 1, 2).start()

        @pl.when(source & (g < LSTEPS))
        def _():
            spread(g * 4 * LCH, 4 * LCH)
            for t in range(4):
                x = sf[pl.ds(2 * t, 4 * LCH, stride=8), :].astype(BF16)
                lraw[pl.ds(pl.multiple_of(g * 4 * LCH, 4 * LCH), 4 * LCH), t * 128:(t + 1) * 128] = x

        for k in range(2):
            chunk = g - hops[k]

            @pl.when((chunk >= 0) & (chunk < LSTEPS))
            def _():
                @pl.when(plain)
                def _():
                    l_copy(own[k], chunk, sibling, s_send.at[k]).wait_recv()

                for dim in range(4):
                    @pl.when(sends[k][dim])
                    def _():
                        push(own[k], chunk, nears[dim], l_send.at[k, dim])

                @pl.when(to_sibling)
                def _():
                    push(own[k], chunk, sibling, s_send.at[k])

        for k in range(2):
            chunk = g - other_hops[k]

            @pl.when((chunk >= 0) & (chunk < LSTEPS))
            def _():
                @pl.when(plain)
                def _():
                    l_copy(others[k], chunk, sibling, s_send.at[2 + k]).wait_recv()

                @pl.when(source)
                def _():
                    push(others[k], chunk, sibling, s_send.at[2 + k])

        @pl.when(g <= INVERT)
        def _():
            @pl.when(g == 0)
            def _():
                for step in range(1, NZ):
                    z_copy(step).start()
                dz[z] = d_ref[...]

            @pl.when(g == DSTEP)
            def _():
                for step in range(1, NZ):
                    z_copy(step).wait()
                dt[core * 16 + node] = jnp.concatenate([dz[i] for i in range(NZ)], axis=1)
                d_copy(0).start()

            for dim in range(1, 5):
                @pl.when(g == (DSTEP + DHOP * dim))
                def _():
                    d_copy(dim - 1).wait()
                    d_copy(dim).start()

            @pl.when(g == INVERT)
            def _():
                d_copy(4).wait()
                for block in range(32):
                    dtf[pl.ds(block_column(block) * 16, 16), :] = dt[block].astype(F32)
                packed = dtf[...].T
                row = lax.broadcasted_iota(jnp.int32, (NB, NB), 0)
                column = lax.broadcasted_iota(jnp.int32, (NB, NB), 1)
                uinv[...] = jnp.where(column >= row, packed, 0.0).astype(BF16)
                linv[...] = jnp.where(column < row, packed, jnp.where(column == row, 1.0, 0.0)).astype(BF16)

        @pl.when(g == early)
        def _():
            solve_u(near_t)
            solve_u(near_t + 1)

        part = g - solve

        @pl.when((part >= 0) & (part < LSTEPS) & (lax.rem(part, 2) == 1))
        def _():
            first = pl.multiple_of(lax.div(part, 2) * PAIR, PAIR)
            rows = pl.ds(first, PAIR)
            l = jnp.dot(lraw[rows, :], uinv[...], preferred_element_type=F32).astype(BF16)
            lsol[rows, :] = l
            update(near_t, first, PAIR, l)
            update(near_t + 1, first, PAIR, l)

            @pl.when(source)
            def _():
                for t in range(4):
                    s_ref[pl.ds(first * 8 + 2 * t, PAIR, stride=8), :] = -l[:, t * 128:(t + 1) * 128].astype(F32)

        @pl.when((g >= late) & (g < late + ROWS // BLK // PER))
        def _():
            @pl.when(g == late)
            def _():
                solve_u(far_t + 1)

            for i in range(PER):
                update_block(far_t + 1, (g - late) * PER + i)

        return carry

    lax.fori_loop(0, TOTAL, step_body, 0)

    solve_u(far_t)

    def last_body(b, carry):
        update_block(far_t, b)
        return carry

    lax.fori_loop(0, ROWS // BLK, last_body, 0)

    @pl.when(z == 0)
    def _():
        for t in range(4):
            s_ref[pl.ds(2 * t, NB, stride=8), :] = jnp.where(source, 0.0, -ub[t, :, 0:128].astype(F32))
            s_ref[pl.ds(2 * t + 1, NB, stride=8), :] = -ub[t, :, 128:256].astype(F32)

    for last in range(SLOTS):
        for way, hop in ways:
            @pl.when(hop != NZ - 1)
            def _():
                u_copy(way, last).wait_send()

            @pl.when(lax.rem(hop, 2) == 0)
            def _():
                u_copy(way, last, 2, 1).wait_send()

                @pl.when(hop != 0)
                def _():
                    u_copy(way, last, NZ - 1, 2).wait_send()

        for k in range(2):
            for dim in range(4):
                @pl.when(sends[k][dim])
                def _():
                    l_copy(own[k], last, nears[dim], l_send.at[k, dim]).wait_send()

            @pl.when(to_sibling)
            def _():
                l_copy(own[k], last, sibling, s_send.at[k]).wait_send()

            @pl.when(source)
            def _():
                l_copy(others[k], last, sibling, s_send.at[2 + k]).wait_send()


def settle(s_ref, a_ref, out_ref, buf, sem):
    z = lax.axis_index("prow")
    source = lax.axis_index("pcol") == 0
    even = lax.broadcasted_iota(jnp.int32, (8, 128), 0) % 2 == 0
    size = OUT * 8

    def copy(b):
        rows = pl.ds(pl.multiple_of(b * size, size), size)
        return pltpu.make_async_copy(buf.at[rows], out_ref.at[rows], sem.at[b])

    def body(b, carry):
        head = (z == 0) & (b < NB // OUT)
        keep_even = jnp.where(head == source, 1.0, 0.0)
        keep_odd = jnp.where(head, 0.0, 1.0)
        keep = jnp.where(even, keep_even, keep_odd)
        rows = pl.ds(pl.multiple_of(b * size, size), size)
        a = a_ref[rows, :].astype(F32).reshape(OUT, 8, 128) * keep[None]
        buf[rows, :] = (a.reshape(size, 128) - s_ref[rows, :]).astype(BF16)
        copy(b).start()
        return carry

    def finish(b, carry):
        copy(b).wait()
        return carry

    lax.fori_loop(0, ROWS // OUT, body, 0)
    lax.fori_loop(0, ROWS // OUT, finish, 0)


def shards(matrix, diag_inverses):
    flat = matrix.reshape(ROWS, 2, 4, 128).transpose(0, 2, 1, 3).reshape(ROWS * 8, 128)
    dma = pltpu.SemaphoreType.DMA
    vmem = pl.BlockSpec(memory_space=pltpu.VMEM)
    product = pl.pallas_call(
        kernel,
        out_shape=jax.ShapeDtypeStruct((ROWS * 8, 128), F32),
        in_specs=[vmem, vmem],
        out_specs=vmem,
        scratch_shapes=[
            pltpu.VMEM((4 * LCH * 8, 128), F32),
            pltpu.VMEM((ROWS, NB), BF16),
            pltpu.VMEM((ROWS, NB), BF16),
            pltpu.VMEM((4, NB, 256), BF16),
            pltpu.VMEM((4, NB, 256), BF16),
            pltpu.VMEM((NB, NB), BF16),
            pltpu.VMEM((NB, NB), BF16),
            pltpu.VMEM((NZ, 16, 64), BF16),
            pltpu.VMEM((32, 16, NB), BF16),
            pltpu.VMEM((NB, NB), F32),
            dma((2, 4, SLOTS)),
            dma((4, LSTEPS)),
            dma((4, SLOTS)),
            dma((3, 2, SLOTS)),
            dma((2, STEPS)),
            dma((NZ - 1,)),
            dma((NZ - 1,)),
            dma((5,)),
            dma((5,)),
        ],
        compiler_params=pltpu.CompilerParams(
            collective_id=0, has_side_effects=True, vmem_limit_bytes=20 * 2**20),
    )(flat, diag_inverses.T)
    out = pl.pallas_call(
        settle,
        out_shape=jax.ShapeDtypeStruct((ROWS * 8, 128), BF16),
        in_specs=[vmem, vmem],
        out_specs=pl.BlockSpec(memory_space=pl.ANY),
        scratch_shapes=[pltpu.VMEM((ROWS * 8, 128), BF16), dma((ROWS // OUT,))],
        compiler_params=pltpu.CompilerParams(vmem_limit_bytes=12 * 2**20),
    )(product, flat)
    return out.reshape(ROWS, 4, 2, 128).transpose(0, 2, 1, 3).reshape(matrix.shape)


def solution(mesh):
    in_specs = (P(None, "prow", None, "pcol"), P("prow", "pcol"))
    out_specs = P(None, "prow", None, "pcol")
    return jax.shard_map(shards, mesh=mesh, in_specs=in_specs, out_specs=out_specs, check_vma=False)
```

```python
import functools

import jax
import jax.numpy as jnp
from jax import lax
from jax.experimental import pallas as pl
from jax.experimental.pallas import tpu as pltpu
from jax.sharding import PartitionSpec as P

MESH = pl.DeviceIdType.MESH
BF16, F32 = jnp.bfloat16, jnp.float32
NB = 512
ROWS = 6 * NB
NZ = 8
STEPS = 16
LSTEPS = 12
LCH = ROWS // (4 * LSTEPS)
UCH = 2 * NB // STEPS
UPER = NB // UCH
BLK = 512
UHOP, LHOP, CHOP = 6, 6, 3
SLOTS = 4
TOTAL = STEPS + (NZ - 1) * UHOP
DSTEP, DHOP = 6, 6
INVERT = DSTEP + 2 * DHOP + 3
OUT = 256
ITEMS = 3 * (ROWS // BLK)
PER = 3


def parent(tree, node):
    bit = 1 << tree
    if not node & bit:
        return node | bit
    if node == bit:
        return 0
    for step in range(1, 4):
        other = 1 << ((tree + step) % 4)
        if node & other:
            return node ^ other


def depth(tree, node):
    return 0 if node == 0 else 1 + depth(tree, parent(tree, node))


def table(bits):
    return sum(1 << node for node in range(16) if bits(node))


CHILD = [[table(lambda v: v ^ (1 << j) and parent(i, v ^ (1 << j)) == v) for j in range(4)] for i in range(4)]
DEPTH = [[table(lambda v: (depth(i, v) >> b) & 1) for b in range(3)] for i in range(4)]


def gray_position(code):
    return code ^ (code >> 1)


def block_column(block):
    core, node = divmod(block, 16)
    return gray_position(node % 4) * 8 + gray_position(node // 4) * 2 + core


def kernel(a_ref, d_ref, s_low, s_high, av, sf, lraw, lsol, uraw, ub, uinv, linv, dz, dt, dtf,
           a_sem, l_send, l_recv, s_send, u_send, u_recv, z_send, z_recv, d_send, d_recv):
    z = lax.axis_index("prow")
    col = lax.axis_index("pcol")
    core = col % 2
    gx, gy = col // 8, (col // 2) % 4
    gx = gx ^ (gx >> 1)
    gy = gy ^ (gy >> 1)
    node = gx + 4 * gy
    sibling = col + 1 - 2 * core
    source = col == 0
    plain = col != 0

    def place(px, py):
        return (px ^ (px >> 1)) * 8 + (py ^ (py >> 1)) * 2 + core

    across = {k: place(gx ^ k, gy) for k in range(1, 4)}
    across.update({4 + k: place(gx, gy ^ k) for k in range(1, 4)})
    nears = [across[1], across[2], across[5], across[6]]

    def look(first, second):
        return (jnp.where(core == 0, first, second) >> node) & 1

    def load_a(piece):
        rows = pl.ds(pl.multiple_of(piece * (NB * 8), NB * 8), NB * 8)
        return pltpu.make_async_copy(a_ref.at[rows], av.at[rows], a_sem.at[piece])

    for piece in range(6):
        load_a(piece).start()

    barrier = pltpu.get_barrier_semaphore()
    for step in range(1, NZ):
        pl.semaphore_signal(barrier, inc=1, device_id=((z + step) % NZ, col), device_id_type=MESH)
    for other in list(across.values()) + [sibling]:
        pl.semaphore_signal(barrier, inc=1, device_id=(z, other), device_id_type=MESH)
    pl.semaphore_wait(barrier, NZ + 6)

    def z_copy(step):
        return pltpu.make_async_remote_copy(
            src_ref=d_ref, dst_ref=dz.at[z], send_sem=z_send.at[step - 1], recv_sem=z_recv.at[step - 1],
            device_id=((z + step) % NZ, col), device_id_type=MESH)

    def d_copy(stage, k=1):
        if stage == 0:
            blocks, target = pl.ds(core * 16 + node, 1), across[k]
        elif stage == 1:
            blocks, target = pl.ds(core * 16 + gy * 4, 4), across[4 + k]
        else:
            blocks, target = pl.ds(core * 16, 16), sibling
        return pltpu.make_async_remote_copy(
            src_ref=dt.at[blocks], dst_ref=dt.at[blocks], send_sem=d_send.at[stage, k], recv_sem=d_recv.at[stage, k],
            device_id=(z, target), device_id_type=MESH)

    def u_copy(way, chunk):
        target = (z + 1) % NZ if way == 0 else (z + NZ - 1) % NZ
        rows = pl.ds(pl.multiple_of(lax.rem(chunk, UPER) * UCH, UCH), UCH)
        part = uraw.at[2 * way + lax.div(chunk, UPER), rows]
        return pltpu.make_async_remote_copy(
            src_ref=part, dst_ref=part, send_sem=u_send.at[way, lax.rem(chunk, SLOTS)], recv_sem=u_recv.at[way, chunk],
            device_id=(target, col), device_id_type=MESH)

    def l_copy(tree, chunk, target, sem):
        part = lraw.at[pl.ds(pl.multiple_of((chunk * 4 + tree) * LCH, LCH), LCH)]
        return pltpu.make_async_remote_copy(
            src_ref=part, dst_ref=part, send_sem=sem.at[lax.rem(chunk, SLOTS)], recv_sem=l_recv.at[tree, chunk],
            device_id=(z, target), device_id_type=MESH)

    def push(tree, chunk, target, sem):
        @pl.when(chunk >= SLOTS)
        def _():
            l_copy(tree, chunk - SLOTS, target, sem).wait_send()

        l_copy(tree, chunk, target, sem).start()

    def spread(first, rows):
        first = pl.multiple_of(first * 8, 16)
        sf[pl.ds(0, rows * 8), :] = av[pl.ds(first, rows * 8), :].astype(F32)

    hop_plus, hop_minus = z, (NZ - z) % NZ
    ways = ((0, hop_plus), (1, hop_minus))

    own, sends, hops = [], [], []
    others, other_hops = [], []
    for k in range(2):
        own.append(2 * core + k)
        sends.append([look(CHILD[k][dim], CHILD[2 + k][dim]) == 1 for dim in range(4)])
        hops.append(sum(look(DEPTH[k][b], DEPTH[2 + k][b]) << b for b in range(3)) * LHOP + core * CHOP)
        others.append(2 * (1 - core) + k)
        hop = sum(look(DEPTH[2 + k][b], DEPTH[k][b]) << b for b in range(3))
        other_hops.append(jnp.where(source, 0, hop * LHOP + (2 - core) * CHOP))
    to_sibling = jnp.logical_not((node == 0) & (core == 1))
    near_hop = jnp.minimum(hop_plus, hop_minus)
    middle = z == NZ // 2
    early = jnp.maximum(INVERT, jnp.where(middle, UPER, STEPS) + near_hop * UHOP)
    solve = jnp.maximum(early, functools.reduce(jnp.maximum, hops + other_hops) + BLK // (4 * LCH) - 1)
    late = jnp.maximum(solve + ITEMS, UPER + jnp.maximum(hop_plus, hop_minus) * UHOP)
    near_t = jnp.where(z <= NZ // 2, 0, 2)
    far_t = 2 - near_t
    order = [near_t, jnp.where(middle, 2, near_t + 1), jnp.where(middle, 1, far_t), far_t + 1]

    def solve_u(t):
        ub[t] = jnp.dot(linv[...], uraw[t], preferred_element_type=F32).astype(BF16)

    def store(first, offset, value):
        for half, ref in enumerate((s_low, s_high)):
            @pl.when((first >= ROWS // 2) == (half == 1))
            def _():
                ref[pl.ds((first - half * (ROWS // 2)) * 8 + offset, BLK, stride=8), :] = value

    def update(t, first, l):
        p = jnp.dot(l, ub[t], preferred_element_type=F32)

        @pl.when(plain)
        def _():
            store(first, 2 * t, p[:, 0:128])

        store(first, 2 * t + 1, p[:, 128:256])

    def update_block(t, b):
        first = pl.multiple_of(b * BLK, BLK)
        update(t, first, lsol[pl.ds(first, BLK), :])

    load_a(0).wait()

    def step_body(g, carry):
        @pl.when((z == 0) & (g < UPER))
        def _():
            spread(g * UCH, UCH)
            for t in range(4):
                for j in range(2):
                    x = sf[pl.ds(2 * t + j, UCH, stride=8), :].astype(BF16)
                    uraw[t, pl.ds(pl.multiple_of(g * UCH, UCH), UCH), j * 128:(j + 1) * 128] = x

        for way, hop in ways:
            chunk = g - hop * UHOP

            @pl.when((chunk >= 0) & (chunk < STEPS))
            def _():
                @pl.when(z != 0)
                def _():
                    u_copy(way, chunk).wait_recv()

                @pl.when(hop != NZ - 1)
                def _():
                    @pl.when(chunk >= SLOTS)
                    def _():
                        u_copy(way, chunk - SLOTS).wait_send()

                    u_copy(way, chunk).start()

        @pl.when(source & (g < LSTEPS))
        def _():
            spread(g * 4 * LCH, 4 * LCH)
            for t in range(4):
                x = sf[pl.ds(2 * t, 4 * LCH, stride=8), :].astype(BF16)
                lraw[pl.ds(pl.multiple_of(g * 4 * LCH, 4 * LCH), 4 * LCH), t * 128:(t + 1) * 128] = x

        for k in range(2):
            chunk = g - hops[k]

            @pl.when((chunk >= 0) & (chunk < LSTEPS))
            def _():
                @pl.when(plain)
                def _():
                    l_copy(own[k], chunk, sibling, s_send.at[k]).wait_recv()

                for dim in range(4):
                    @pl.when(sends[k][dim])
                    def _():
                        push(own[k], chunk, nears[dim], l_send.at[k, dim])

                @pl.when(to_sibling)
                def _():
                    push(own[k], chunk, sibling, s_send.at[k])

        for k in range(2):
            chunk = g - other_hops[k]

            @pl.when((chunk >= 0) & (chunk < LSTEPS))
            def _():
                @pl.when(plain)
                def _():
                    l_copy(others[k], chunk, sibling, s_send.at[2 + k]).wait_recv()

                @pl.when(source)
                def _():
                    push(others[k], chunk, sibling, s_send.at[2 + k])

        @pl.when(g <= INVERT)
        def _():
            @pl.when((g >= 1) & (g < 6))
            def _():
                load_a(g).wait()

            @pl.when(g == 0)
            def _():
                for step in range(1, NZ):
                    z_copy(step).start()
                dz[z] = d_ref[...]

            @pl.when(g == DSTEP)
            def _():
                for step in range(1, NZ):
                    z_copy(step).wait()
                dt[core * 16 + node] = jnp.concatenate([dz[i] for i in range(NZ)], axis=1)
                for k in range(1, 4):
                    d_copy(0, k).start()

            @pl.when(g == DSTEP + DHOP)
            def _():
                for k in range(1, 4):
                    d_copy(0, k).wait()
                for k in range(1, 4):
                    d_copy(1, k).start()

            @pl.when(g == DSTEP + 2 * DHOP)
            def _():
                for k in range(1, 4):
                    d_copy(1, k).wait()
                d_copy(2).start()

            @pl.when(g == INVERT)
            def _():
                d_copy(2).wait()
                for block in range(32):
                    dtf[pl.ds(block_column(block) * 16, 16), :] = dt[block].astype(F32)
                packed = dtf[...].T
                row = lax.broadcasted_iota(jnp.int32, (NB, NB), 0)
                column = lax.broadcasted_iota(jnp.int32, (NB, NB), 1)
                uinv[...] = jnp.where(column >= row, packed, 0.0).astype(BF16)
                linv[...] = jnp.where(column < row, packed, jnp.where(column == row, 1.0, 0.0)).astype(BF16)

        @pl.when(g == early)
        def _():
            solve_u(order[0])
            solve_u(order[1])

        part = g - solve

        @pl.when((part >= 0) & (part < ITEMS))
        def _():
            block, item = lax.div(part, 3), lax.rem(part, 3)

            @pl.when(item == 0)
            def _():
                first = pl.multiple_of(block * BLK, BLK)
                rows = pl.ds(first, BLK)
                l = jnp.dot(lraw[rows, :], uinv[...], preferred_element_type=F32).astype(BF16)
                lsol[rows, :] = l

                @pl.when(source)
                def _():
                    for t in range(4):
                        store(first, 2 * t, -l[:, t * 128:(t + 1) * 128].astype(F32))

            @pl.when(item != 0)
            def _():
                update_block(jnp.where(item == 1, order[0], order[1]), block)

        @pl.when((g >= late) & (g < late + ROWS // BLK // PER))
        def _():
            @pl.when(g == late)
            def _():
                solve_u(order[2])

            for i in range(PER):
                update_block(order[2], (g - late) * PER + i)

        return carry

    lax.fori_loop(0, TOTAL, step_body, 0)

    solve_u(order[3])

    def last_body(b, carry):
        update_block(order[3], b)
        return carry

    lax.fori_loop(0, ROWS // BLK, last_body, 0)

    @pl.when(z == 0)
    def _():
        for t in range(4):
            s_low[pl.ds(2 * t, NB, stride=8), :] = jnp.where(source, 0.0, -ub[t, :, 0:128].astype(F32))
            s_low[pl.ds(2 * t + 1, NB, stride=8), :] = -ub[t, :, 128:256].astype(F32)

    for last in range(SLOTS):
        for way, hop in ways:
            @pl.when(hop != NZ - 1)
            def _():
                u_copy(way, last).wait_send()

        for k in range(2):
            for dim in range(4):
                @pl.when(sends[k][dim])
                def _():
                    l_copy(own[k], last, nears[dim], l_send.at[k, dim]).wait_send()

            @pl.when(to_sibling)
            def _():
                l_copy(own[k], last, sibling, s_send.at[k]).wait_send()

            @pl.when(source)
            def _():
                l_copy(others[k], last, sibling, s_send.at[2 + k]).wait_send()


def settle(s_low, s_high, a_ref, out_ref, buf, sem):
    z = lax.axis_index("prow")
    source = lax.axis_index("pcol") == 0
    even = lax.broadcasted_iota(jnp.int32, (8, 128), 0) % 2 == 0
    size = OUT * 8

    def copy(b):
        rows = pl.ds(pl.multiple_of(b * size, size), size)
        return pltpu.make_async_copy(buf.at[rows], out_ref.at[rows], sem.at[b])

    def body(s_ref, first, b, carry):
        head = (z == 0) & (b < NB // OUT)
        keep_even = jnp.where(head == source, 1.0, 0.0)
        keep_odd = jnp.where(head, 0.0, 1.0)
        keep = jnp.where(even, keep_even, keep_odd)
        rows = pl.ds(pl.multiple_of(b * size, size), size)
        a = a_ref[rows, :].astype(F32).reshape(OUT, 8, 128) * keep[None]
        part = pl.ds(pl.multiple_of((b - first) * size, size), size)
        buf[rows, :] = (a.reshape(size, 128) - s_ref[part, :]).astype(BF16)
        copy(b).start()
        return carry

    def finish(b, carry):
        copy(b).wait()
        return carry

    half = ROWS // OUT // 2
    lax.fori_loop(0, half, functools.partial(body, s_low, 0), 0)
    lax.fori_loop(half, 2 * half, functools.partial(body, s_high, half), 0)
    lax.fori_loop(0, ROWS // OUT, finish, 0)


def shards(matrix, diag_inverses):
    flat = matrix.reshape(ROWS, 2, 4, 128).transpose(0, 2, 1, 3).reshape(ROWS * 8, 128)
    dma = pltpu.SemaphoreType.DMA
    vmem = pl.BlockSpec(memory_space=pltpu.VMEM)
    low, high, a = pl.pallas_call(
        kernel,
        out_shape=[
            jax.ShapeDtypeStruct((ROWS * 4, 128), F32),
            jax.ShapeDtypeStruct((ROWS * 4, 128), F32),
            jax.ShapeDtypeStruct((ROWS * 8, 128), BF16),
        ],
        in_specs=[pl.BlockSpec(memory_space=pltpu.HBM), vmem],
        out_specs=[vmem] * 3,
        scratch_shapes=[
            pltpu.VMEM((4 * LCH * 8, 128), F32),
            pltpu.VMEM((ROWS, NB), BF16),
            pltpu.VMEM((ROWS, NB), BF16),
            pltpu.VMEM((4, NB, 256), BF16),
            pltpu.VMEM((4, NB, 256), BF16),
            pltpu.VMEM((NB, NB), BF16),
            pltpu.VMEM((NB, NB), BF16),
            pltpu.VMEM((NZ, 16, 64), BF16),
            pltpu.VMEM((32, 16, NB), BF16),
            pltpu.VMEM((NB, NB), F32),
            dma((6,)),
            dma((2, 4, SLOTS)),
            dma((4, LSTEPS)),
            dma((4, SLOTS)),
            dma((2, SLOTS)),
            dma((2, STEPS)),
            dma((NZ - 1,)),
            dma((NZ - 1,)),
            dma((3, 4)),
            dma((3, 4)),
        ],
        compiler_params=pltpu.CompilerParams(
            collective_id=0, has_side_effects=True, vmem_limit_bytes=33 * 2**20),
    )(flat, diag_inverses.T)
    out = pl.pallas_call(
        settle,
        out_shape=jax.ShapeDtypeStruct((ROWS * 8, 128), BF16),
        in_specs=[vmem] * 3,
        out_specs=pl.BlockSpec(memory_space=pl.ANY),
        scratch_shapes=[pltpu.VMEM((ROWS * 8, 128), BF16), dma((ROWS // OUT,))],
        compiler_params=pltpu.CompilerParams(vmem_limit_bytes=12 * 2**20),
    )(low, high, a)
    return out.reshape(ROWS, 4, 2, 128).transpose(0, 2, 1, 3).reshape(matrix.shape)


def solution(mesh):
    in_specs = (P(None, "prow", None, "pcol"), P("prow", "pcol"))
    out_specs = P(None, "prow", None, "pcol")
    return jax.shard_map(shards, mesh=mesh, in_specs=in_specs, out_specs=out_specs, check_vma=False)
```

```python
import functools

import jax
import jax.numpy as jnp
from jax import lax
from jax.experimental import pallas as pl
from jax.experimental.pallas import tpu as pltpu
from jax.sharding import PartitionSpec as P

MESH = pl.DeviceIdType.MESH
BF16, F32 = jnp.bfloat16, jnp.float32
NB = 512
ROWS = 6 * NB
NZ = 8
STEPS = 16
LSTEPS = 12
LCH = ROWS // (4 * LSTEPS)
UCH = 2 * NB // STEPS
UPER = NB // UCH
BLK = 512
UHOP, LHOP, CHOP = 5, 5, 2
SLOTS = 4
TOTAL = STEPS + (NZ - 1) * UHOP
DSTEP, DHOP = 6, 6
INVERT = DSTEP + 2 * DHOP + 3
OUT = 256
ITEMS = 3 * (ROWS // BLK)
PER = 3


def parent(tree, node):
    bit = 1 << tree
    if not node & bit:
        return node | bit
    if node == bit:
        return 0
    for step in range(1, 4):
        other = 1 << ((tree + step) % 4)
        if node & other:
            return node ^ other


def depth(tree, node):
    return 0 if node == 0 else 1 + depth(tree, parent(tree, node))


def table(bits):
    return sum(1 << node for node in range(16) if bits(node))


CHILD = [[table(lambda v: v ^ (1 << j) and parent(i, v ^ (1 << j)) == v) for j in range(4)] for i in range(4)]
DEPTH = [[table(lambda v: (depth(i, v) >> b) & 1) for b in range(3)] for i in range(4)]


def gray_position(code):
    return code ^ (code >> 1)


def block_column(block):
    core, node = divmod(block, 16)
    return gray_position(node % 4) * 8 + gray_position(node // 4) * 2 + core


def kernel(a_ref, d_ref, s_low, s_high, av, sf, lraw, lsol, uraw, ub, uinv, linv, dz, dt, dtf,
           a_sem, l_send, l_recv, s_send, u_send, u_recv, z_send, z_recv, d_send, d_recv):
    z = lax.axis_index("prow")
    col = lax.axis_index("pcol")
    core = col % 2
    gx, gy = col // 8, (col // 2) % 4
    gx = gx ^ (gx >> 1)
    gy = gy ^ (gy >> 1)
    node = gx + 4 * gy
    sibling = col + 1 - 2 * core
    source = col == 0
    plain = col != 0

    def place(px, py):
        return (px ^ (px >> 1)) * 8 + (py ^ (py >> 1)) * 2 + core

    across = {k: place(gx ^ k, gy) for k in range(1, 4)}
    across.update({4 + k: place(gx, gy ^ k) for k in range(1, 4)})
    nears = [across[1], across[2], across[5], across[6]]

    def look(first, second):
        return (jnp.where(core == 0, first, second) >> node) & 1

    def load_a(piece):
        rows = pl.ds(pl.multiple_of(piece * (NB * 8), NB * 8), NB * 8)
        return pltpu.make_async_copy(a_ref.at[rows], av.at[rows], a_sem.at[piece])

    for piece in range(6):
        load_a(piece).start()

    barrier = pltpu.get_barrier_semaphore()
    for step in range(1, NZ):
        pl.semaphore_signal(barrier, inc=1, device_id=((z + step) % NZ, col), device_id_type=MESH)
    for other in list(across.values()) + [sibling]:
        pl.semaphore_signal(barrier, inc=1, device_id=(z, other), device_id_type=MESH)
    pl.semaphore_wait(barrier, NZ + 6)

    def z_copy(step):
        return pltpu.make_async_remote_copy(
            src_ref=d_ref, dst_ref=dz.at[z], send_sem=z_send.at[step - 1], recv_sem=z_recv.at[step - 1],
            device_id=((z + step) % NZ, col), device_id_type=MESH)

    def d_copy(stage, k=1):
        if stage == 0:
            blocks, target = pl.ds(core * 16 + node, 1), across[k]
        elif stage == 1:
            blocks, target = pl.ds(core * 16 + gy * 4, 4), across[4 + k]
        else:
            blocks, target = pl.ds(core * 16, 16), sibling
        return pltpu.make_async_remote_copy(
            src_ref=dt.at[blocks], dst_ref=dt.at[blocks], send_sem=d_send.at[stage, k], recv_sem=d_recv.at[stage, k],
            device_id=(z, target), device_id_type=MESH)

    def u_copy(way, chunk):
        target = (z + 1) % NZ if way == 0 else (z + NZ - 1) % NZ
        rows = pl.ds(pl.multiple_of(lax.rem(chunk, UPER) * UCH, UCH), UCH)
        part = uraw.at[2 * way + lax.div(chunk, UPER), rows]
        return pltpu.make_async_remote_copy(
            src_ref=part, dst_ref=part, send_sem=u_send.at[way, lax.rem(chunk, SLOTS)], recv_sem=u_recv.at[way, chunk],
            device_id=(target, col), device_id_type=MESH)

    def l_copy(tree, chunk, target, sem):
        part = lraw.at[pl.ds(pl.multiple_of((chunk * 4 + tree) * LCH, LCH), LCH)]
        return pltpu.make_async_remote_copy(
            src_ref=part, dst_ref=part, send_sem=sem.at[lax.rem(chunk, SLOTS)], recv_sem=l_recv.at[tree, chunk],
            device_id=(z, target), device_id_type=MESH)

    def push(tree, chunk, target, sem):
        @pl.when(chunk >= SLOTS)
        def _():
            l_copy(tree, chunk - SLOTS, target, sem).wait_send()

        l_copy(tree, chunk, target, sem).start()

    def spread(first, rows):
        first = pl.multiple_of(first * 8, 16)
        sf[pl.ds(0, rows * 8), :] = av[pl.ds(first, rows * 8), :].astype(F32)

    hop_plus, hop_minus = z, (NZ - z) % NZ
    ways = ((0, hop_plus), (1, hop_minus))

    own, sends, hops = [], [], []
    others, other_hops = [], []
    for k in range(2):
        own.append(2 * core + k)
        sends.append([look(CHILD[k][dim], CHILD[2 + k][dim]) == 1 for dim in range(4)])
        hops.append(sum(look(DEPTH[k][b], DEPTH[2 + k][b]) << b for b in range(3)) * LHOP + core * CHOP)
        others.append(2 * (1 - core) + k)
        hop = sum(look(DEPTH[2 + k][b], DEPTH[k][b]) << b for b in range(3))
        other_hops.append(jnp.where(source, 0, hop * LHOP + (2 - core) * CHOP))
    to_sibling = jnp.logical_not((node == 0) & (core == 1))
    near_hop = jnp.minimum(hop_plus, hop_minus)
    middle = z == NZ // 2
    early = jnp.maximum(INVERT, jnp.where(middle, UPER, STEPS) + near_hop * UHOP)
    solve = jnp.maximum(early, functools.reduce(jnp.maximum, hops + other_hops) + BLK // (4 * LCH) - 1)
    late = jnp.maximum(solve + ITEMS, UPER + jnp.maximum(hop_plus, hop_minus) * UHOP)
    near_t = jnp.where(z <= NZ // 2, 0, 2)
    far_t = 2 - near_t
    order = [near_t, jnp.where(middle, 2, near_t + 1), jnp.where(middle, 1, far_t), far_t + 1]

    def solve_u(slot):
        u = jnp.dot(linv[...], uraw[order[slot]], preferred_element_type=F32).astype(BF16)
        ub[slot // 2, :, slot % 2 * 256:slot % 2 * 256 + 256] = u

    def store(first, offset, value):
        for half, ref in enumerate((s_low, s_high)):
            @pl.when((first >= ROWS // 2) == (half == 1))
            def _():
                ref[pl.ds((first - half * (ROWS // 2)) * 8 + offset, BLK, stride=8), :] = value

    def update(b, slots):
        first = pl.multiple_of(b * BLK, BLK)
        low = slots[0] % 2 * 256
        u = ub[slots[0] // 2, :, low:low + 256 * len(slots)]
        p = jnp.dot(lsol[pl.ds(first, BLK), :], u, preferred_element_type=F32)

        @pl.when(plain)
        def _():
            for i, slot in enumerate(slots):
                store(first, 2 * order[slot], p[:, i * 256:i * 256 + 128])

        for i, slot in enumerate(slots):
            store(first, 2 * order[slot] + 1, p[:, i * 256 + 128:i * 256 + 256])

    load_a(0).wait()

    def step_body(g, carry):
        @pl.when((z == 0) & (g < UPER))
        def _():
            spread(g * UCH, UCH)
            for t in range(4):
                for j in range(2):
                    x = sf[pl.ds(2 * t + j, UCH, stride=8), :].astype(BF16)
                    uraw[t, pl.ds(pl.multiple_of(g * UCH, UCH), UCH), j * 128:(j + 1) * 128] = x

        for way, hop in ways:
            chunk = g - hop * UHOP

            @pl.when((chunk >= 0) & (chunk < STEPS))
            def _():
                @pl.when(z != 0)
                def _():
                    u_copy(way, chunk).wait_recv()

                @pl.when(hop != NZ - 1)
                def _():
                    @pl.when(chunk >= SLOTS)
                    def _():
                        u_copy(way, chunk - SLOTS).wait_send()

                    u_copy(way, chunk).start()

        @pl.when(source & (g < LSTEPS))
        def _():
            spread(g * 4 * LCH, 4 * LCH)
            for t in range(4):
                x = sf[pl.ds(2 * t, 4 * LCH, stride=8), :].astype(BF16)
                lraw[pl.ds(pl.multiple_of(g * 4 * LCH, 4 * LCH), 4 * LCH), t * 128:(t + 1) * 128] = x

        for k in range(2):
            chunk = g - hops[k]

            @pl.when((chunk >= 0) & (chunk < LSTEPS))
            def _():
                @pl.when(plain)
                def _():
                    l_copy(own[k], chunk, sibling, s_send.at[k]).wait_recv()

                for dim in range(4):
                    @pl.when(sends[k][dim])
                    def _():
                        push(own[k], chunk, nears[dim], l_send.at[k, dim])

                @pl.when(to_sibling)
                def _():
                    push(own[k], chunk, sibling, s_send.at[k])

        for k in range(2):
            chunk = g - other_hops[k]

            @pl.when((chunk >= 0) & (chunk < LSTEPS))
            def _():
                @pl.when(plain)
                def _():
                    l_copy(others[k], chunk, sibling, s_send.at[2 + k]).wait_recv()

                @pl.when(source)
                def _():
                    push(others[k], chunk, sibling, s_send.at[2 + k])

        @pl.when(g <= INVERT)
        def _():
            @pl.when((g >= 1) & (g < 6))
            def _():
                load_a(g).wait()

            @pl.when(g == 0)
            def _():
                for step in range(1, NZ):
                    z_copy(step).start()
                dz[z] = d_ref[...]

            @pl.when(g == DSTEP)
            def _():
                for step in range(1, NZ):
                    z_copy(step).wait()
                dt[core * 16 + node] = jnp.concatenate([dz[i] for i in range(NZ)], axis=1)
                for k in range(1, 4):
                    d_copy(0, k).start()

            @pl.when(g == DSTEP + DHOP)
            def _():
                for k in range(1, 4):
                    d_copy(0, k).wait()
                for k in range(1, 4):
                    d_copy(1, k).start()

            @pl.when(g == DSTEP + 2 * DHOP)
            def _():
                for k in range(1, 4):
                    d_copy(1, k).wait()
                d_copy(2).start()

            @pl.when(g == INVERT)
            def _():
                d_copy(2).wait()
                for block in range(32):
                    dtf[pl.ds(block_column(block) * 16, 16), :] = dt[block].astype(F32)
                packed = dtf[...].T
                row = lax.broadcasted_iota(jnp.int32, (NB, NB), 0)
                column = lax.broadcasted_iota(jnp.int32, (NB, NB), 1)
                uinv[...] = jnp.where(column >= row, packed, 0.0).astype(BF16)
                linv[...] = jnp.where(column < row, packed, jnp.where(column == row, 1.0, 0.0)).astype(BF16)

        @pl.when(g == early)
        def _():
            solve_u(0)
            solve_u(1)

        part = g - solve

        @pl.when((part >= 0) & (part < ITEMS))
        def _():
            block, item = lax.div(part, 3), lax.rem(part, 3)

            @pl.when(item == 0)
            def _():
                first = pl.multiple_of(block * BLK, BLK)
                rows = pl.ds(first, BLK)
                l = jnp.dot(lraw[rows, :], uinv[...], preferred_element_type=F32).astype(BF16)
                lsol[rows, :] = l

                @pl.when(source)
                def _():
                    for t in range(4):
                        store(first, 2 * t, -l[:, t * 128:(t + 1) * 128].astype(F32))

            for slot in range(2):
                @pl.when(item == slot + 1)
                def _():
                    update(block, (slot,))

        @pl.when((g >= late) & (g < late + ROWS // BLK // PER))
        def _():
            @pl.when(g == late)
            def _():
                solve_u(2)

            for i in range(PER):
                update((g - late) * PER + i, (2,))

        return carry

    lax.fori_loop(0, TOTAL, step_body, 0)

    solve_u(3)

    last_t = order[3]
    for b in range(ROWS // BLK):
        ref, first = (s_low, b * BLK) if b < ROWS // BLK // 2 else (s_high, b * BLK - ROWS // 2)
        p = jnp.dot(lsol[b * BLK:(b + 1) * BLK, :], ub[1, :, 256:512], preferred_element_type=F32)
        for j in range(2):
            ref[pl.ds(first * 8 + 2 * last_t + j, BLK, stride=8), :] = p[:, j * 128:(j + 1) * 128]

    @pl.when(source)
    def _():
        lanes = pl.ds(pl.multiple_of(last_t * 128, 128), 128)
        for half, ref in enumerate((s_low, s_high)):
            l = lsol[pl.ds(half * (ROWS // 2), ROWS // 2), lanes].astype(F32)
            ref[pl.ds(2 * last_t, ROWS // 2, stride=8), :] = -l

    @pl.when(z == 0)
    def _():
        for t in range(4):
            s_low[pl.ds(2 * t, NB, stride=8), :] = jnp.where(source, 0.0, -ub[t // 2, :, t % 2 * 256:t % 2 * 256 + 128].astype(F32))
            s_low[pl.ds(2 * t + 1, NB, stride=8), :] = -ub[t // 2, :, t % 2 * 256 + 128:t % 2 * 256 + 256].astype(F32)

    for last in range(SLOTS):
        for way, hop in ways:
            @pl.when(hop != NZ - 1)
            def _():
                u_copy(way, last).wait_send()

        for k in range(2):
            for dim in range(4):
                @pl.when(sends[k][dim])
                def _():
                    l_copy(own[k], last, nears[dim], l_send.at[k, dim]).wait_send()

            @pl.when(to_sibling)
            def _():
                l_copy(own[k], last, sibling, s_send.at[k]).wait_send()

            @pl.when(source)
            def _():
                l_copy(others[k], last, sibling, s_send.at[2 + k]).wait_send()


def settle(s_low, s_high, a_ref, out_ref, buf, sem):
    z = lax.axis_index("prow")
    source = lax.axis_index("pcol") == 0
    even = lax.broadcasted_iota(jnp.int32, (8, 128), 0) % 2 == 0
    size = OUT * 8

    def copy(b):
        rows = pl.ds(pl.multiple_of(b * size, size), size)
        return pltpu.make_async_copy(buf.at[rows], out_ref.at[rows], sem.at[b])

    def body(s_ref, first, b, carry):
        head = (z == 0) & (b < NB // OUT)
        keep_even = jnp.where(head == source, 1.0, 0.0)
        keep_odd = jnp.where(head, 0.0, 1.0)
        keep = jnp.where(even, keep_even, keep_odd)
        rows = pl.ds(pl.multiple_of(b * size, size), size)
        a = a_ref[rows, :].astype(F32).reshape(OUT, 8, 128) * keep[None]
        part = pl.ds(pl.multiple_of((b - first) * size, size), size)
        buf[rows, :] = (a.reshape(size, 128) - s_ref[part, :]).astype(BF16)
        copy(b).start()
        return carry

    def finish(b, carry):
        copy(b).wait()
        return carry

    half = ROWS // OUT // 2
    lax.fori_loop(0, half, functools.partial(body, s_low, 0), 0)
    lax.fori_loop(half, 2 * half, functools.partial(body, s_high, half), 0)
    lax.fori_loop(0, ROWS // OUT, finish, 0)


def shards(matrix, diag_inverses):
    flat = matrix.reshape(ROWS, 2, 4, 128).transpose(0, 2, 1, 3).reshape(ROWS * 8, 128)
    dma = pltpu.SemaphoreType.DMA
    vmem = pl.BlockSpec(memory_space=pltpu.VMEM)
    low, high, a = pl.pallas_call(
        kernel,
        out_shape=[
            jax.ShapeDtypeStruct((ROWS * 4, 128), F32),
            jax.ShapeDtypeStruct((ROWS * 4, 128), F32),
            jax.ShapeDtypeStruct((ROWS * 8, 128), BF16),
        ],
        in_specs=[pl.BlockSpec(memory_space=pltpu.HBM), vmem],
        out_specs=[vmem] * 3,
        scratch_shapes=[
            pltpu.VMEM((4 * LCH * 8, 128), F32),
            pltpu.VMEM((ROWS, NB), BF16),
            pltpu.VMEM((ROWS, NB), BF16),
            pltpu.VMEM((4, NB, 256), BF16),
            pltpu.VMEM((2, NB, NB), BF16),
            pltpu.VMEM((NB, NB), BF16),
            pltpu.VMEM((NB, NB), BF16),
            pltpu.VMEM((NZ, 16, 64), BF16),
            pltpu.VMEM((32, 16, NB), BF16),
            pltpu.VMEM((NB, NB), F32),
            dma((6,)),
            dma((2, 4, SLOTS)),
            dma((4, LSTEPS)),
            dma((4, SLOTS)),
            dma((2, SLOTS)),
            dma((2, STEPS)),
            dma((NZ - 1,)),
            dma((NZ - 1,)),
            dma((3, 4)),
            dma((3, 4)),
        ],
        compiler_params=pltpu.CompilerParams(
            collective_id=0, has_side_effects=True, vmem_limit_bytes=33 * 2**20),
    )(flat, diag_inverses.T)
    out = pl.pallas_call(
        settle,
        out_shape=jax.ShapeDtypeStruct((ROWS * 8, 128), BF16),
        in_specs=[vmem] * 3,
        out_specs=pl.BlockSpec(memory_space=pl.ANY),
        scratch_shapes=[pltpu.VMEM((ROWS * 8, 128), BF16), dma((ROWS // OUT,))],
        compiler_params=pltpu.CompilerParams(vmem_limit_bytes=12 * 2**20),
    )(low, high, a)
    return out.reshape(ROWS, 4, 2, 128).transpose(0, 2, 1, 3).reshape(matrix.shape)


def solution(mesh):
    in_specs = (P(None, "prow", None, "pcol"), P("prow", "pcol"))
    out_specs = P(None, "prow", None, "pcol")
    return jax.shard_map(shards, mesh=mesh, in_specs=in_specs, out_specs=out_specs, check_vma=False)
```

```python
import functools

import jax
import jax.numpy as jnp
from jax import lax
from jax.experimental import pallas as pl
from jax.experimental.pallas import tpu as pltpu
from jax.sharding import PartitionSpec as P

MESH = pl.DeviceIdType.MESH
BF16, F32 = jnp.bfloat16, jnp.float32
NB = 512
ROWS = 6 * NB
NZ = 8
STEPS = 16
LSTEPS = 12
LCH = ROWS // (4 * LSTEPS)
UCH = 2 * NB // STEPS
UPER = NB // UCH
BLK = 512
UHOP, LHOP, CHOP = 4, 4, 2
SLOTS = 4
TOTAL = max(STEPS + (NZ - 1) * UHOP, STEPS + NZ // 2 * UHOP + 3 * ROWS // NB)
DSTEP, DHOP = 6, 6
INVERT = DSTEP + 2 * DHOP + 3
OUT = 256
ITEMS = 3 * (ROWS // BLK)


def parent(tree, node):
    bit = 1 << tree
    if not node & bit:
        return node | bit
    if node == bit:
        return 0
    for step in range(1, 4):
        other = 1 << ((tree + step) % 4)
        if node & other:
            return node ^ other


def depth(tree, node):
    return 0 if node == 0 else 1 + depth(tree, parent(tree, node))


def table(bits):
    return sum(1 << node for node in range(16) if bits(node))


CHILD = [[table(lambda v: v ^ (1 << j) and parent(i, v ^ (1 << j)) == v) for j in range(4)] for i in range(4)]
DEPTH = [[table(lambda v: (depth(i, v) >> b) & 1) for b in range(3)] for i in range(4)]


def gray_position(code):
    return code ^ (code >> 1)


def block_column(block):
    core, node = divmod(block, 16)
    return gray_position(node % 4) * 8 + gray_position(node // 4) * 2 + core


def kernel(a_ref, d_ref, s_low, s_high, av, sf, lraw, lsol, uraw, ub, uinv, linv, dz, dt, dtf,
           a_sem, l_send, l_recv, s_send, u_send, u_recv, z_send, z_recv, d_send, d_recv):
    z = lax.axis_index("prow")
    col = lax.axis_index("pcol")
    core = col % 2
    gx, gy = col // 8, (col // 2) % 4
    gx = gx ^ (gx >> 1)
    gy = gy ^ (gy >> 1)
    node = gx + 4 * gy
    sibling = col + 1 - 2 * core
    source = col == 0
    plain = col != 0

    def place(px, py):
        return (px ^ (px >> 1)) * 8 + (py ^ (py >> 1)) * 2 + core

    across = {k: place(gx ^ k, gy) for k in range(1, 4)}
    across.update({4 + k: place(gx, gy ^ k) for k in range(1, 4)})
    nears = [across[1], across[2], across[5], across[6]]

    def look(first, second):
        return (jnp.where(core == 0, first, second) >> node) & 1

    def load_a(piece):
        rows = pl.ds(pl.multiple_of(piece * (NB * 8), NB * 8), NB * 8)
        return pltpu.make_async_copy(a_ref.at[rows], av.at[rows], a_sem.at[piece])

    for piece in range(6):
        load_a(piece).start()

    barrier = pltpu.get_barrier_semaphore()
    for step in range(1, NZ):
        pl.semaphore_signal(barrier, inc=1, device_id=((z + step) % NZ, col), device_id_type=MESH)
    for other in list(across.values()) + [sibling]:
        pl.semaphore_signal(barrier, inc=1, device_id=(z, other), device_id_type=MESH)
    pl.semaphore_wait(barrier, NZ + 6)

    def z_copy(step):
        return pltpu.make_async_remote_copy(
            src_ref=d_ref, dst_ref=dz.at[z], send_sem=z_send.at[step - 1], recv_sem=z_recv.at[step - 1],
            device_id=((z + step) % NZ, col), device_id_type=MESH)

    def d_copy(stage, k=1):
        if stage == 0:
            blocks, target = pl.ds(core * 16 + node, 1), across[k]
        elif stage == 1:
            blocks, target = pl.ds(core * 16 + gy * 4, 4), across[4 + k]
        else:
            blocks, target = pl.ds(core * 16, 16), sibling
        return pltpu.make_async_remote_copy(
            src_ref=dt.at[blocks], dst_ref=dt.at[blocks], send_sem=d_send.at[stage, k], recv_sem=d_recv.at[stage, k],
            device_id=(z, target), device_id_type=MESH)

    def u_copy(way, chunk):
        target = (z + 1) % NZ if way == 0 else (z + NZ - 1) % NZ
        rows = pl.ds(pl.multiple_of(lax.rem(chunk, UPER) * UCH, UCH), UCH)
        part = uraw.at[2 * way + lax.div(chunk, UPER), rows]
        return pltpu.make_async_remote_copy(
            src_ref=part, dst_ref=part, send_sem=u_send.at[way, lax.rem(chunk, SLOTS)], recv_sem=u_recv.at[way, chunk],
            device_id=(target, col), device_id_type=MESH)

    def l_copy(tree, chunk, target, sem):
        part = lraw.at[pl.ds(pl.multiple_of((chunk * 4 + tree) * LCH, LCH), LCH)]
        return pltpu.make_async_remote_copy(
            src_ref=part, dst_ref=part, send_sem=sem.at[lax.rem(chunk, SLOTS)], recv_sem=l_recv.at[tree, chunk],
            device_id=(z, target), device_id_type=MESH)

    def push(tree, chunk, target, sem):
        @pl.when(chunk >= SLOTS)
        def _():
            l_copy(tree, chunk - SLOTS, target, sem).wait_send()

        l_copy(tree, chunk, target, sem).start()

    def spread(first, rows):
        first = pl.multiple_of(first * 8, 16)
        sf[pl.ds(0, rows * 8), :] = av[pl.ds(first, rows * 8), :].astype(F32)

    hop_plus, hop_minus = z, (NZ - z) % NZ
    ways = ((0, hop_plus), (1, hop_minus))

    own, sends, hops = [], [], []
    others, other_hops = [], []
    for k in range(2):
        own.append(2 * core + k)
        sends.append([look(CHILD[k][dim], CHILD[2 + k][dim]) == 1 for dim in range(4)])
        hops.append(sum(look(DEPTH[k][b], DEPTH[2 + k][b]) << b for b in range(3)) * LHOP + core * CHOP)
        others.append(2 * (1 - core) + k)
        hop = sum(look(DEPTH[2 + k][b], DEPTH[k][b]) << b for b in range(3))
        other_hops.append(jnp.where(source, 0, hop * LHOP + (2 - core) * CHOP))
    to_sibling = jnp.logical_not((node == 0) & (core == 1))
    near_hop = jnp.minimum(hop_plus, hop_minus)
    middle = z == NZ // 2
    early = jnp.maximum(INVERT, jnp.where(middle, UPER, STEPS) + near_hop * UHOP)
    solve = jnp.maximum(early, functools.reduce(jnp.maximum, hops + other_hops) + BLK // (4 * LCH) - 1)
    late = jnp.maximum(solve + ITEMS, UPER + jnp.maximum(hop_plus, hop_minus) * UHOP)
    near_t = jnp.where(z <= NZ // 2, 0, 2)
    far_t = 2 - near_t
    order = [near_t, jnp.where(middle, 2, near_t + 1), jnp.where(middle, 1, far_t), far_t + 1]

    def solve_u(slot):
        u = jnp.dot(linv[...], uraw[order[slot]], preferred_element_type=F32).astype(BF16)
        ub[slot // 2, :, slot % 2 * 256:slot % 2 * 256 + 256] = u

    def store(first, offset, value):
        for half, ref in enumerate((s_low, s_high)):
            @pl.when((first >= ROWS // 2) == (half == 1))
            def _():
                ref[pl.ds((first - half * (ROWS // 2)) * 8 + offset, BLK, stride=8), :] = value

    def update(b, slots):
        first = pl.multiple_of(b * BLK, BLK)
        low = slots[0] % 2 * 256
        u = ub[slots[0] // 2, :, low:low + 256 * len(slots)]
        p = jnp.dot(lsol[pl.ds(first, BLK), :], u, preferred_element_type=F32)

        @pl.when(plain)
        def _():
            for i, slot in enumerate(slots):
                store(first, 2 * order[slot], p[:, i * 256:i * 256 + 128])

        for i, slot in enumerate(slots):
            store(first, 2 * order[slot] + 1, p[:, i * 256 + 128:i * 256 + 256])

    def quarter(slot):
        low = slot % 2 * 256
        for b in range(ROWS // BLK):
            ref, first = (s_low, b * BLK) if b < ROWS // BLK // 2 else (s_high, b * BLK - ROWS // 2)
            u = ub[slot // 2, :, low:low + 256]
            p = jnp.dot(lsol[b * BLK:(b + 1) * BLK, :], u, preferred_element_type=F32)
            for j in range(2):
                ref[pl.ds(first * 8 + 2 * order[slot] + j, BLK, stride=8), :] = p[:, j * 128:(j + 1) * 128]

    load_a(0).wait()

    def step_body(g, carry):
        @pl.when((z == 0) & (g < UPER))
        def _():
            spread(g * UCH, UCH)
            for t in range(4):
                for j in range(2):
                    x = sf[pl.ds(2 * t + j, UCH, stride=8), :].astype(BF16)
                    uraw[t, pl.ds(pl.multiple_of(g * UCH, UCH), UCH), j * 128:(j + 1) * 128] = x

        for way, hop in ways:
            chunk = g - hop * UHOP

            @pl.when((chunk >= 0) & (chunk < STEPS))
            def _():
                @pl.when(z != 0)
                def _():
                    u_copy(way, chunk).wait_recv()

                @pl.when(hop != NZ - 1)
                def _():
                    @pl.when(chunk >= SLOTS)
                    def _():
                        u_copy(way, chunk - SLOTS).wait_send()

                    u_copy(way, chunk).start()

        @pl.when(source & (g < LSTEPS))
        def _():
            spread(g * 4 * LCH, 4 * LCH)
            for t in range(4):
                x = sf[pl.ds(2 * t, 4 * LCH, stride=8), :].astype(BF16)
                lraw[pl.ds(pl.multiple_of(g * 4 * LCH, 4 * LCH), 4 * LCH), t * 128:(t + 1) * 128] = x

        for k in range(2):
            chunk = g - hops[k]

            @pl.when((chunk >= 0) & (chunk < LSTEPS))
            def _():
                @pl.when(plain)
                def _():
                    l_copy(own[k], chunk, sibling, s_send.at[k]).wait_recv()

                for dim in range(4):
                    @pl.when(sends[k][dim])
                    def _():
                        push(own[k], chunk, nears[dim], l_send.at[k, dim])

                @pl.when(to_sibling)
                def _():
                    push(own[k], chunk, sibling, s_send.at[k])

        for k in range(2):
            chunk = g - other_hops[k]

            @pl.when((chunk >= 0) & (chunk < LSTEPS))
            def _():
                @pl.when(plain)
                def _():
                    l_copy(others[k], chunk, sibling, s_send.at[2 + k]).wait_recv()

                @pl.when(source)
                def _():
                    push(others[k], chunk, sibling, s_send.at[2 + k])

        @pl.when(g <= INVERT)
        def _():
            @pl.when((g >= 1) & (g < 6))
            def _():
                load_a(g).wait()

            @pl.when(g == 0)
            def _():
                for step in range(1, NZ):
                    z_copy(step).start()
                dz[z] = d_ref[...]

            @pl.when(g == DSTEP)
            def _():
                for step in range(1, NZ):
                    z_copy(step).wait()
                dt[core * 16 + node] = jnp.concatenate([dz[i] for i in range(NZ)], axis=1)
                for k in range(1, 4):
                    d_copy(0, k).start()

            @pl.when(g == DSTEP + DHOP)
            def _():
                for k in range(1, 4):
                    d_copy(0, k).wait()
                for k in range(1, 4):
                    d_copy(1, k).start()

            @pl.when(g == DSTEP + 2 * DHOP)
            def _():
                for k in range(1, 4):
                    d_copy(1, k).wait()
                d_copy(2).start()

            @pl.when(g == INVERT)
            def _():
                d_copy(2).wait()
                for block in range(32):
                    dtf[pl.ds(block_column(block) * 16, 16), :] = dt[block].astype(F32)
                packed = dtf[...].T
                row = lax.broadcasted_iota(jnp.int32, (NB, NB), 0)
                column = lax.broadcasted_iota(jnp.int32, (NB, NB), 1)
                uinv[...] = jnp.where(column >= row, packed, 0.0).astype(BF16)
                linv[...] = jnp.where(column < row, packed, jnp.where(column == row, 1.0, 0.0)).astype(BF16)

        @pl.when(g == early)
        def _():
            solve_u(0)
            solve_u(1)

        part = g - solve

        @pl.when((part >= 0) & (part < ITEMS))
        def _():
            block, item = lax.div(part, 3), lax.rem(part, 3)

            @pl.when(item == 0)
            def _():
                first = pl.multiple_of(block * BLK, BLK)
                rows = pl.ds(first, BLK)
                l = jnp.dot(lraw[rows, :], uinv[...], preferred_element_type=F32).astype(BF16)
                lsol[rows, :] = l

                @pl.when(source)
                def _():
                    for t in range(4):
                        store(first, 2 * t, -l[:, t * 128:(t + 1) * 128].astype(F32))

            for slot in range(2):
                @pl.when(item == slot + 1)
                def _():
                    update(block, (slot,))

        @pl.when(g == late)
        def _():
            solve_u(2)
            quarter(2)

        return carry

    lax.fori_loop(0, TOTAL, step_body, 0)

    solve_u(3)

    quarter(3)

    @pl.when(source)
    def _():
        for slot in (2, 3):
            t = order[slot]
            lanes = pl.ds(pl.multiple_of(t * 128, 128), 128)
            for half, ref in enumerate((s_low, s_high)):
                l = lsol[pl.ds(half * (ROWS // 2), ROWS // 2), lanes].astype(F32)
                ref[pl.ds(2 * t, ROWS // 2, stride=8), :] = -l

    @pl.when(z == 0)
    def _():
        for t in range(4):
            s_low[pl.ds(2 * t, NB, stride=8), :] = jnp.where(source, 0.0, -ub[t // 2, :, t % 2 * 256:t % 2 * 256 + 128].astype(F32))
            s_low[pl.ds(2 * t + 1, NB, stride=8), :] = -ub[t // 2, :, t % 2 * 256 + 128:t % 2 * 256 + 256].astype(F32)

    for last in range(SLOTS):
        for way, hop in ways:
            @pl.when(hop != NZ - 1)
            def _():
                u_copy(way, last).wait_send()

        for k in range(2):
            for dim in range(4):
                @pl.when(sends[k][dim])
                def _():
                    l_copy(own[k], last, nears[dim], l_send.at[k, dim]).wait_send()

            @pl.when(to_sibling)
            def _():
                l_copy(own[k], last, sibling, s_send.at[k]).wait_send()

            @pl.when(source)
            def _():
                l_copy(others[k], last, sibling, s_send.at[2 + k]).wait_send()


def settle(s_low, s_high, a_ref, out_ref, buf, sem):
    z = lax.axis_index("prow")
    source = lax.axis_index("pcol") == 0
    even = lax.broadcasted_iota(jnp.int32, (8, 128), 0) % 2 == 0
    size = OUT * 8

    def copy(b):
        rows = pl.ds(pl.multiple_of(b * size, size), size)
        return pltpu.make_async_copy(buf.at[rows], out_ref.at[rows], sem.at[b])

    def body(s_ref, first, b, carry):
        head = (z == 0) & (b < NB // OUT)
        keep_even = jnp.where(head == source, 1.0, 0.0)
        keep_odd = jnp.where(head, 0.0, 1.0)
        keep = jnp.where(even, keep_even, keep_odd)
        rows = pl.ds(pl.multiple_of(b * size, size), size)
        a = a_ref[rows, :].astype(F32).reshape(OUT, 8, 128) * keep[None]
        part = pl.ds(pl.multiple_of((b - first) * size, size), size)
        buf[rows, :] = (a.reshape(size, 128) - s_ref[part, :]).astype(BF16)
        copy(b).start()
        return carry

    def finish(b, carry):
        copy(b).wait()
        return carry

    half = ROWS // OUT // 2
    lax.fori_loop(0, half, functools.partial(body, s_low, 0), 0)
    lax.fori_loop(half, 2 * half, functools.partial(body, s_high, half), 0)
    lax.fori_loop(0, ROWS // OUT, finish, 0)


def shards(matrix, diag_inverses):
    flat = matrix.reshape(ROWS, 2, 4, 128).transpose(0, 2, 1, 3).reshape(ROWS * 8, 128)
    dma = pltpu.SemaphoreType.DMA
    vmem = pl.BlockSpec(memory_space=pltpu.VMEM)
    low, high, a = pl.pallas_call(
        kernel,
        out_shape=[
            jax.ShapeDtypeStruct((ROWS * 4, 128), F32),
            jax.ShapeDtypeStruct((ROWS * 4, 128), F32),
            jax.ShapeDtypeStruct((ROWS * 8, 128), BF16),
        ],
        in_specs=[pl.BlockSpec(memory_space=pltpu.HBM), vmem],
        out_specs=[vmem] * 3,
        scratch_shapes=[
            pltpu.VMEM((4 * LCH * 8, 128), F32),
            pltpu.VMEM((ROWS, NB), BF16),
            pltpu.VMEM((ROWS, NB), BF16),
            pltpu.VMEM((4, NB, 256), BF16),
            pltpu.VMEM((2, NB, NB), BF16),
            pltpu.VMEM((NB, NB), BF16),
            pltpu.VMEM((NB, NB), BF16),
            pltpu.VMEM((NZ, 16, 64), BF16),
            pltpu.VMEM((32, 16, NB), BF16),
            pltpu.VMEM((NB, NB), F32),
            dma((6,)),
            dma((2, 4, SLOTS)),
            dma((4, LSTEPS)),
            dma((4, SLOTS)),
            dma((2, SLOTS)),
            dma((2, STEPS)),
            dma((NZ - 1,)),
            dma((NZ - 1,)),
            dma((3, 4)),
            dma((3, 4)),
        ],
        compiler_params=pltpu.CompilerParams(
            collective_id=0, has_side_effects=True, vmem_limit_bytes=33 * 2**20),
    )(flat, diag_inverses.T)
    out = pl.pallas_call(
        settle,
        out_shape=jax.ShapeDtypeStruct((ROWS * 8, 128), BF16),
        in_specs=[vmem] * 3,
        out_specs=pl.BlockSpec(memory_space=pl.ANY),
        scratch_shapes=[pltpu.VMEM((ROWS * 8, 128), BF16), dma((ROWS // OUT,))],
        compiler_params=pltpu.CompilerParams(vmem_limit_bytes=12 * 2**20),
    )(low, high, a)
    return out.reshape(ROWS, 4, 2, 128).transpose(0, 2, 1, 3).reshape(matrix.shape)


def solution(mesh):
    in_specs = (P(None, "prow", None, "pcol"), P("prow", "pcol"))
    out_specs = P(None, "prow", None, "pcol")
    return jax.shard_map(shards, mesh=mesh, in_specs=in_specs, out_specs=out_specs, check_vma=False)
```
